128 devices in a mesh: seq: 16 (over y, x), dp: 8 (over z, core).
Axes of the slice: x: 4, y: 4, z: 4, core: 2. Of those that a mesh axis runs over, the one named last changes fastest.
Arguments:
- queries: bfloat16 [8, 2048, 4096], P('dp', 'seq'), may hold values from -6 to 12
- image_keys: bfloat16 [8, 16, 1601, 512], P('dp', 'seq'), may hold values from -6 to 12
- image_values: bfloat16 [8, 16, 1601, 512], P('dp', 'seq'), may hold values from -6 to 6
- cotangent: bfloat16 [8, 2048, 4096], P('dp', 'seq'), may hold values from -6 to 6
- gate: float32 [], replicated, may hold values from 0.3 to 1.2
- tile_list: int32 [8, 16, 2], P('dp'), may hold values from 0 to 15, as said below
- slot_range: int32 [8, 2048, 2], P('dp'), may hold values from 0 to 2, as said below
Outputs:
- attended: bfloat16 [8, 2048, 4096], P('dp', 'seq')
- query_grad: bfloat16 [8, 2048, 4096], P('dp', 'seq')
- key_grad: bfloat16 [8, 16, 1601, 512], P('dp', 'seq')
- value_grad: bfloat16 [8, 16, 1601, 512], P('dp', 'seq')
- gate_grad: float32 [], replicated
The draws below stay inside these ranges and needn't reach their ends.
Inputs may be any that keep to these rules, and one draw needn't show every extreme that they name: `tile_list`: each row lists 2 different tiles of its batch. Tile g of a batch is held by the device at index g // 1 of seq, and block b stands on the device at index b of seq. A block's first listed tile is held by its own device, its second by a device whose index differs from its own by one. At most 3 blocks of one batch list the same tile, and in every batch some tile is listed by exactly 3 blocks. `slot_range`: for every token the first value is at most the second. A range may be empty, and a listed slot may be attended by no token of its block.
All inputs are finite; a program needn't handle non-finite values.
Results may differ from the reference program's by a relative error of at most 0.0075.
The reference program's roundings to bfloat16 on the way count: a program that leaves them out, or rounds other values in their place, can miss the bound.
Values may be sent and summed in bfloat16 or wider, within the bound.
A program may use at most 192 MiB of HBM per device.

```python
import jax
import jax.numpy as jnp
from jax import lax

KV_HEADS = 4
HEAD_DIM = 128
BLOCK = 128
TILE_TOK = 1601
MAXT = 2
TILE_DEV = 1
GROUP = 8
QW = 4096
KW = 512
BATCHES = 8
BLOCKS = 16
TOKENS = 2048
TILES = 16


def draw_queries(key, part):
    key = jax.random.fold_in(key, 11)
    shape = (BATCHES, TOKENS, QW)
    values = jnp.clip(jax.random.normal(key, shape, jnp.float32), -6.0, 6.0)
    return values.astype(jnp.bfloat16)


def draw_image_keys(key, part):
    key = jax.random.fold_in(key, 17)
    shape = (BATCHES, TILES, TILE_TOK, KW)
    values = jnp.clip(jax.random.normal(key, shape, jnp.float32), -6.0, 6.0)
    return values.astype(jnp.bfloat16)


def draw_tile_list(key, part):
    key = jax.random.fold_in(key, 29)
    shape = (BATCHES, BLOCKS)
    block = jnp.arange(BLOCKS)[None, :]
    own = block * TILE_DEV + jax.random.randint(jax.random.fold_in(key, 1), shape, 0, TILE_DEV)
    side = jnp.where(jax.random.randint(jax.random.fold_in(key, 2), shape, 0, 2) == 0, -1, 1)
    side = jnp.where(block == BLOCKS - 1, -1, side)
    side = jnp.where(block == 0, 1, side)
    side = jnp.where(block == 2, -1, side)
    other = (block + side) * TILE_DEV + jax.random.randint(jax.random.fold_in(key, 3), shape, 0, TILE_DEV)
    own = jnp.where(block == 1, TILE_DEV, own)
    other = jnp.where((block == 0) | (block == 2), TILE_DEV, other)
    return jnp.stack([own, other], axis=-1).astype(jnp.int32)


def draw_slot_range(key, part):
    key = jax.random.fold_in(key, 23)
    count = BATCHES * TOKENS // BLOCK
    first = jax.random.randint(jax.random.fold_in(key, 1), (count, 1), 1, BLOCK // 2 + 1)
    second = first + jax.random.randint(jax.random.fold_in(key, 2), (count, 1), 0, BLOCK // 4 + 1)
    skipped = jax.random.randint(jax.random.fold_in(key, 3), (count, 1), 0, 3) == 0
    skipped = skipped & (jnp.arange(count)[:, None] > 0)
    position = jnp.arange(BLOCK)[None, :]
    lower = jnp.where(position < first, jnp.where(skipped, 1, 0), 1)
    upper = jnp.where(position < first, MAXT, jnp.where(position < second, 1, MAXT))
    both = jnp.stack([lower, upper], axis=-1).astype(jnp.int32)
    return both.reshape(BATCHES, TOKENS, 2)


def levels(key, dims, pieces, smallest, largest):
    def one(dim, blocks):
        draws = jax.random.uniform(jax.random.fold_in(jax.random.fold_in(key, 6), dim), (blocks,), jnp.float32, smallest / len(pieces), largest / len(pieces))
        return jnp.repeat(jnp.exp(draws), dims[dim] // blocks).reshape((-1,) + (1,) * (len(dims) - dim - 1))

    level = one(*pieces[0])
    for cut in pieces[1:]:
        level = level * one(*cut)
    return level


def noise(rng, shape, deviation, most, split=(), dtype=jnp.bfloat16):
    drawn = jax.random.normal(rng, shape, jnp.float32) * deviation
    if len(split) > 0:
        drawn = levels(rng, shape, split, -0.22, 0.18) * drawn
    return jnp.clip(drawn, min=-most, max=most).astype(dtype)


def setup_inputs(seed: int = 0) -> dict:
    splits = jax.random.split(jax.random.key(seed), 8)
    queries = draw_queries(jax.random.fold_in(splits[7], 71), 0)
    image_keys = draw_image_keys(jax.random.fold_in(splits[7], 71), 0)
    image_values = noise(splits[2], (BATCHES, TILES, TILE_TOK, KW), 1.0, 6.0, ((0, 8), (1, 16)))
    cotangent = noise(splits[3], (BATCHES, TOKENS, QW), 1.0, 6.0, ((0, 8), (1, 16)))
    gate = jnp.clip(jax.random.uniform(splits[4], (), jnp.float32, 0.3, 1.2), 0.3, 1.2)
    tile_list = draw_tile_list(jax.random.fold_in(splits[7], 71), 0)
    slot_range = draw_slot_range(jax.random.fold_in(splits[7], 71), 0)
    return dict(queries=queries, image_keys=image_keys, image_values=image_values, cotangent=cotangent, gate=gate, tile_list=tile_list, slot_range=slot_range)


NEG_FILL = -1.0e30


def settle(values):
    return lax.optimization_barrier(values.astype(jnp.bfloat16)).astype(jnp.float32)


def fetch_tile(table, tile):
    picked = lax.dynamic_index_in_dim(table, tile.astype(jnp.int32), 0, keepdims=False)
    return picked.astype(jnp.float32).reshape(TILE_TOK, KV_HEADS, HEAD_DIM)


def add_tile(table, tile, update):
    index = tile.astype(jnp.int32)
    former = lax.dynamic_index_in_dim(table, index, 0, keepdims=False)
    return lax.dynamic_update_index_in_dim(table, former + update.reshape(TILE_TOK, KW), index, 0)


def batch_pass(queries, image_keys, image_values, cotangent, tile_list, slot_range, gate_tanh):
    scale = HEAD_DIM ** -0.5
    count = TOKENS // BLOCK
    query_blocks = queries.reshape(count, BLOCK, QW)
    grad_blocks = cotangent.reshape(count, BLOCK, QW)
    range_blocks = slot_range.reshape(count, BLOCK, 2)

    def advance(carry, item):
        key_acc, value_acc = carry
        query_block, grad_block, row_range, listed = item
        q_heads = query_block.astype(jnp.float32).reshape(BLOCK, KV_HEADS, GROUP, HEAD_DIM)
        masks, key_tiles, value_tiles, maxima, totals, partials = [], [], [], [], [], []
        for slot in range(MAXT):
            key_tile = fetch_tile(image_keys, listed[slot])
            value_tile = fetch_tile(image_values, listed[slot])
            active = ((row_range[:, 0] <= slot) & (slot < row_range[:, 1]))[:, None, None]
            scores = jnp.einsum("tkgd,skd->tkgs", q_heads, key_tile) * scale
            row_max = jnp.where(active, jnp.max(scores, axis=-1), NEG_FILL)
            probs = jnp.where(active[..., None], jnp.exp(scores - row_max[..., None]), 0.0)
            total = jnp.sum(probs, axis=-1)
            numerator = jnp.einsum("tkgs,skd->tkgd", settle(probs), value_tile)
            partial_out = jnp.where(active[..., None], numerator / jnp.where(active, total, 1.0)[..., None], 0.0)
            masks.append(active)
            key_tiles.append(key_tile)
            value_tiles.append(value_tile)
            maxima.append(row_max)
            totals.append(total)
            partials.append(partial_out)
        top = maxima[0]
        for row_max in maxima[1:]:
            top = jnp.maximum(top, row_max)
        shares = [total * jnp.exp(row_max - top) for total, row_max in zip(totals, maxima)]
        whole = shares[0]
        merged = shares[0][..., None] * partials[0]
        for share, partial_out in zip(shares[1:], partials[1:]):
            whole = whole + share
            merged = merged + share[..., None] * partial_out
        any_active = (row_range[:, 0] < row_range[:, 1])[:, None, None]
        combined = jnp.where(any_active[..., None], merged / jnp.where(any_active, whole, 1.0)[..., None], 0.0)
        lse = jnp.where(any_active, top + jnp.log(jnp.where(any_active, whole, 1.0)), 0.0)
        attended = (gate_tanh * combined).reshape(BLOCK, QW).astype(jnp.bfloat16)
        d_out = settle(gate_tanh * grad_block.astype(jnp.float32)).reshape(BLOCK, KV_HEADS, GROUP, HEAD_DIM)
        delta = jnp.sum(d_out * combined, axis=-1)
        gate_term = jnp.sum(grad_block.astype(jnp.float32).reshape(combined.shape) * combined)
        query_grad = jnp.zeros_like(combined)
        for slot in range(MAXT):
            active = masks[slot]
            key_tile = key_tiles[slot]
            value_tile = value_tiles[slot]
            scores = jnp.einsum("tkgd,skd->tkgs", q_heads, key_tile) * scale
            back_probs = jnp.where(active[..., None], jnp.exp(scores - lse[..., None]), 0.0)
            value_part = jnp.einsum("tkgs,tkgd->skd", settle(back_probs), d_out)
            prob_grad = jnp.einsum("tkgd,skd->tkgs", d_out, value_tile)
            score_grad = settle(back_probs * (prob_grad - delta[..., None]))
            query_grad = query_grad + settle(jnp.einsum("tkgs,skd->tkgd", score_grad, key_tile) * scale)
            key_part = jnp.einsum("tkgs,tkgd->skd", score_grad, q_heads) * scale
            key_acc = add_tile(key_acc, listed[slot], key_part)
            value_acc = add_tile(value_acc, listed[slot], value_part)
        outputs = (attended, query_grad.reshape(BLOCK, QW).astype(jnp.bfloat16), gate_term)
        return (key_acc, value_acc), outputs

    start = (jnp.zeros((TILES, TILE_TOK, KW), jnp.float32), jnp.zeros((TILES, TILE_TOK, KW), jnp.float32))
    (key_acc, value_acc), (attended, query_grad, gate_terms) = lax.scan(
        advance, start, (query_blocks, grad_blocks, range_blocks, tile_list))
    return (attended.reshape(TOKENS, QW), query_grad.reshape(TOKENS, QW),
            key_acc.astype(jnp.bfloat16), value_acc.astype(jnp.bfloat16), jnp.sum(gate_terms))


def reference(queries, image_keys, image_values, cotangent, gate, tile_list, slot_range):
    gate_tanh = jnp.tanh(gate.astype(jnp.float32))

    def one_batch(items):
        return batch_pass(items[0], items[1], items[2], items[3], items[4], items[5], gate_tanh)

    attended, query_grad, key_grad, value_grad, gate_terms = lax.map(
        one_batch, (queries, image_keys, image_values, cotangent, tile_list, slot_range))
    gate_grad = (1.0 - gate_tanh * gate_tanh) * jnp.sum(gate_terms)
    return attended, query_grad, key_grad, value_grad, gate_grad
```

```python
import functools

import jax
import jax.numpy as jnp
from jax import lax
from jax.experimental import pallas as pl
from jax.experimental.pallas import tpu as pltpu
from jax.sharding import PartitionSpec as P

KV = 4
GROUP = 8
HD = 128
BLK = 128
KEYS = 1601
KEYS_MAIN = 1600
KEYS_ROWS = 1616
KEYS_WIDE = 1664
WIDTH = GROUP * HD
PARTS = 4
ROWS = 2 * BLK
CUTS = ((0, 512), (512, 512), (1024, 512), (1536, 80))
UNITS = 3 * KV
LAG = 4
SLOTS = LAG + 1
LOW = -1e30
SCALE = HD**-0.5
LOG2E = 1.4426950408889634
FACTOR = SCALE * LOG2E
F32 = jnp.float32
BF16 = jnp.bfloat16
MESH = pl.DeviceIdType.MESH
NT = (((1,), (1,)), ((), ()))


def mm(a, b):
    return jnp.dot(a, b, preferred_element_type=F32)


def mm_nt(a, b):
    return lax.dot_general(a, b, NT, preferred_element_type=F32)


def stack_rows(pair):
    return jnp.concatenate([pair[:, :HD], pair[:, HD:]], axis=0)


def turn(pair):
    return jnp.concatenate([pair[:, :HD].T, pair[:, HD:].T], axis=1)


def kernel(
    ring,
    rounds,
    gate_ref,
    mask_ref,
    ktail_ref,
    vtail_ref,
    q_hbm,
    cot_hbm,
    k_hbm,
    v_hbm,
    att_hbm,
    dq_hbm,
    dk_hbm,
    dv_hbm,
    gsum_ref,
    qb,
    cb,
    kp,
    vp,
    kt,
    vt,
    ret_o,
    ret_q,
    own_o,
    onum,
    pbuf,
    dk_acc,
    dv_acc,
    stats,
    stats_out,
    stats_in,
    lse_out,
    lse_in,
    cvec,
    gacc,
    gsend,
    grecv,
    s_kv,
    s_own,
    s_q,
    s_c,
    s_stat,
    s_lse,
    s_ro,
    s_rq,
    s_out,
    s_kvout,
    s_g,
):
    me = lax.axis_index("seq")
    dpi = lax.axis_index("dp")
    right = lax.rem(me + 1, ring)
    left = lax.rem(me + ring - 1, ring)
    tanh = gate_ref[0, 0]

    def cols(h):
        return pl.ds(pl.multiple_of(h * WIDTH, WIDTH), WIDTH)

    def to_side(d):
        return right if d == 0 else left

    def send_q(d, h):
        return pltpu.make_async_remote_copy(
            src_ref=q_hbm.at[:, cols(h)],
            dst_ref=qb.at[d, h],
            send_sem=s_q.at[0, d, h],
            recv_sem=s_q.at[1, d, h],
            device_id={"seq": to_side(d)},
            device_id_type=MESH,
        )

    def send_c(d, h):
        return pltpu.make_async_remote_copy(
            src_ref=cot_hbm.at[:, cols(h)],
            dst_ref=cb.at[d, h],
            send_sem=s_c.at[0, d, h],
            recv_sem=s_c.at[1, d, h],
            device_id={"seq": to_side(d)},
            device_id_type=MESH,
        )

    def send_stat(p, h):
        return pltpu.make_async_remote_copy(
            src_ref=stats_out.at[p, h],
            dst_ref=stats_in.at[1 - p, h],
            send_sem=s_stat.at[0, p, h],
            recv_sem=s_stat.at[1, 1 - p, h],
            device_id={"seq": to_side(1 - p)},
            device_id_type=MESH,
        )

    def send_lse(d, h):
        return pltpu.make_async_remote_copy(
            src_ref=lse_out.at[h],
            dst_ref=lse_in.at[d, h],
            send_sem=s_lse.at[0, d, h],
            recv_sem=s_lse.at[1, d, h],
            device_id={"seq": to_side(d)},
            device_id_type=MESH,
        )

    def send_ro(p, h):
        return pltpu.make_async_remote_copy(
            src_ref=cb.at[p, h],
            dst_ref=ret_o.at[1 - p, h],
            send_sem=s_ro.at[0, p, h],
            recv_sem=s_ro.at[1, 1 - p, h],
            device_id={"seq": to_side(1 - p)},
            device_id_type=MESH,
        )

    def send_rq(p, h):
        return pltpu.make_async_remote_copy(
            src_ref=qb.at[p, h],
            dst_ref=ret_q.at[1 - p, h],
            send_sem=s_rq.at[0, p, h],
            recv_sem=s_rq.at[1, 1 - p, h],
            device_id={"seq": to_side(1 - p)},
            device_id_type=MESH,
        )

    def gate_partner(r):
        name, place, bit = ("seq", me, r) if r < rounds[0] else ("dp", dpi, r - rounds[0])
        stride = 1 << bit
        return {name: place + stride * (1 - 2 * ((place // stride) % 2))}

    def send_gate(r):
        return pltpu.make_async_remote_copy(
            src_ref=gsend.at[r],
            dst_ref=grecv.at[r],
            send_sem=s_g.at[0, r],
            recv_sem=s_g.at[1, r],
            device_id=gate_partner(r),
            device_id_type=MESH,
        )

    own_q = lambda h: pltpu.make_async_copy(q_hbm.at[:, cols(h)], qb.at[2, h], s_own.at[0, h])
    own_c = lambda h: pltpu.make_async_copy(cot_hbm.at[:, cols(h)], cb.at[2, h], s_own.at[1, h])

    def load_kv(which, h):
        src, dst = ((k_hbm, kp), (v_hbm, vp))[which]
        lanes = pl.ds(pl.multiple_of(h * HD, HD), HD)
        return pltpu.make_async_copy(
            src.at[pl.ds(0, KEYS_MAIN), lanes],
            dst.at[h, pl.ds(0, KEYS_MAIN)],
            s_kv.at[which, h],
        )

    def store_kv(which, h):
        src, dst = ((kp, dk_hbm), (vp, dv_hbm))[which]
        return pltpu.make_async_copy(
            src.at[h, pl.ds(0, KEYS_ROWS)], dst.at[h], s_kvout.at[which, h]
        )

    def store_att(h):
        return pltpu.make_async_copy(cb.at[2, h], att_hbm.at[:, cols(h)], s_out.at[0, h])

    def store_dq(h):
        return pltpu.make_async_copy(qb.at[2, h], dq_hbm.at[:, cols(h)], s_out.at[1, h])

    for h in range(KV):
        for which in range(2):
            load_kv(which, h).start()
    for h in range(KV):
        own_q(h).start()
        own_c(h).start()

    total_rounds = rounds[0] + rounds[1]
    barrier = pltpu.get_barrier_semaphore()
    for side in (left, right):
        pl.semaphore_signal(barrier, inc=1, device_id={"seq": side}, device_id_type=MESH)
    for r in range(total_rounds):
        pl.semaphore_signal(barrier, inc=1, device_id=gate_partner(r), device_id_type=MESH)
    pl.semaphore_wait(barrier, 2 + total_rounds)

    for h in range(KV):
        for d in range(2):
            send_q(d, h).start()
        for d in range(2):
            send_c(d, h).start()

    gacc[...] = jnp.zeros_like(gacc)

    def prepare(h, _):
        for which in range(2):
            load_kv(which, h).wait()
        lanes = pl.ds(pl.multiple_of(h * HD, HD), HD)
        for tail, dst, flipped in ((ktail_ref, kp, kt), (vtail_ref, vp, vt)):
            dst[h, KEYS_MAIN:KEYS_ROWS, :] = tail[:, lanes]
            dst[h, KEYS_ROWS:, :] = jnp.zeros((KEYS_WIDE - KEYS_ROWS, HD), BF16)
            for j in range(KEYS_WIDE // HD):
                piece = dst[h, j * HD : (j + 1) * HD, :]
                flipped[h, :, j * HD : (j + 1) * HD] = piece.T
        return 0

    lax.fori_loop(0, KV, prepare, 0)

    def combine(h):
        send_stat(0, h).wait_recv()
        send_stat(1, h).wait_recv()
        mine = stats_out[2, h]
        low = stats_in[0, h]
        high = stats_in[1, h]
        top = jnp.maximum(jnp.maximum(mine[0], low[0]), high[0])
        shares = [one[1] * jnp.exp2(one[0] - top) for one in (mine, low, high)]
        whole = shares[0] + shares[1] + shares[2]
        some = whole > 0.0
        safe = jnp.where(some, whole, 1.0)
        delta = (shares[0] * mine[2] + shares[1] * low[2] + shares[2] * high[2]) / safe
        gamma = (shares[0] * mine[3] + shares[1] * low[3] + shares[2] * high[3]) / safe
        lse_out[h, 0] = jnp.where(some, top + jnp.log(safe) * LOG2E, 0.0)
        lse_out[h, 1] = jnp.where(some, delta, 0.0)
        gacc[...] += jnp.where(some, gamma, 0.0)
        for d in range(2):
            send_lse(d, h).start()

    def finalize(h):
        for p in range(2):
            send_ro(p, h).wait_recv()
            send_rq(p, h).wait_recv()
        cb[2, h] = (own_o[h] + ret_o[0, h].astype(F32) + ret_o[1, h].astype(F32)).astype(BF16)
        qb[2, h] = (
            qb[2, h].astype(F32) + ret_q[0, h].astype(F32) + ret_q[1, h].astype(F32)
        ).astype(BF16)
        store_att(h).start()
        store_dq(h).start()

    def forward_chunk(u, c):
        h, p, slot = u // 3, u % 3, u % SLOTS
        lanes = pl.ds(pl.multiple_of(c * ROWS, ROWS), ROWS)
        query = stack_rows(qb[p, h, :, lanes])
        row_max = None
        for start, size in CUTS:
            scores = mm_nt(kp[h, start : start + size, :], query)
            if start + size > KEYS:
                position = lax.broadcasted_iota(jnp.int32, scores.shape, 0)
                scores = jnp.where(position < KEYS - start, scores, LOW)
            pbuf[slot, c, start : start + size, :] = scores
            part = jnp.max(scores, axis=0, keepdims=True)
            row_max = part if row_max is None else jnp.maximum(row_max, part)
        row_max = row_max * FACTOR
        total = jnp.zeros((1, ROWS), F32)
        out = jnp.zeros((HD, ROWS), F32)
        for start, size in CUTS:
            probs = jnp.exp2(pbuf[slot, c, start : start + size, :] * FACTOR - row_max)
            pbuf[slot, c, start : start + size, :] = probs
            total = total + jnp.sum(probs, axis=0, keepdims=True)
            out = out + mm(vt[h, :, start : start + size], probs.astype(BF16))
        onum[slot, c] = out
        cot = turn(cb[p, h, :, lanes].astype(F32))
        grad = (tanh * cot).astype(BF16).astype(F32)
        delta = jnp.sum(grad * out, axis=0, keepdims=True) / total
        gamma = jnp.sum(cot * out, axis=0, keepdims=True) / total
        for kind, row in enumerate((row_max, total, delta, gamma)):
            for g in range(2):
                stats[slot, kind, pl.ds(2 * c + g, 1), :] = row[:, g * BLK : (g + 1) * BLK]

    def backward_chunk(u, c):
        h, p, slot = u // 3, u % 3, u % SLOTS
        lanes = pl.ds(pl.multiple_of(c * ROWS, ROWS), ROWS)
        query = stack_rows(qb[p, h, :, lanes])
        grad = (tanh * stack_rows(cb[p, h, :, lanes]).astype(F32)).astype(BF16)
        rows = [cvec[i, pl.ds(2 * c + g, 1), :] for i in range(2) for g in range(2)]
        weight = jnp.concatenate(rows[:2], axis=1)
        delta = jnp.concatenate(rows[2:], axis=1)
        turned = jnp.zeros((HD, ROWS), F32)
        for start, size in CUTS:
            keys = slice(start, start + size)
            probs = pbuf[slot, c, keys, :] * weight
            prob_grad = mm_nt(vp[h, keys, :], grad)
            score_grad = (probs * (prob_grad - delta)).astype(BF16)
            dv_acc[keys, :] += mm(probs.astype(BF16), grad)
            dk_acc[keys, :] += mm(score_grad, query)
            turned = turned + mm(kt[h, :, keys], score_grad)
        turned = turned * SCALE
        out = onum[slot, c] * (weight * tanh)
        dq = jnp.concatenate([turned[:, :BLK].T, turned[:, BLK:].T], axis=1).astype(BF16)
        out = jnp.concatenate([out[:, :BLK].T, out[:, BLK:].T], axis=1)
        qb[p, h, :, lanes] = dq

        @pl.when(p < 2)
        def _():
            cb[p, h, :, lanes] = out.astype(BF16)

        @pl.when(p == 2)
        def _():
            own_o[h, :, lanes] = out

    def forward_start(u):
        h, p = u // 3, u % 3

        for d in range(2):

            @pl.when(p == d)
            def _():
                send_q(d, h).wait_recv()
                send_c(d, h).wait_recv()

        @pl.when(p == 2)
        def _():
            own_q(h).wait()
            own_c(h).wait()

    def forward_end(u):
        h, p, slot = u // 3, u % 3, u % SLOTS
        on = mask_ref[p] > 0.0
        for kind, fill in enumerate((LOW, 0.0, 0.0, 0.0)):
            stats_out[p, h, kind] = jnp.where(on, stats[slot, kind], fill)
        for d in range(2):

            @pl.when(p == d)
            def _():
                send_stat(d, h).start()

    def backward_start(u):
        h, p, slot = u // 3, u % 3, u % SLOTS
        on = mask_ref[p] > 0.0
        for d in range(2):

            @pl.when(p == d)
            def _():
                send_lse(d, h).wait_recv()
                cvec[0] = jnp.where(on, jnp.exp2(stats[slot, 0] - lse_in[d, h, 0]), 0.0)
                cvec[1] = lse_in[d, h, 1]

        @pl.when(p == 2)
        def _():
            cvec[0] = jnp.where(on, jnp.exp2(stats[slot, 0] - lse_out[h, 0]), 0.0)
            cvec[1] = lse_out[h, 1]

        @pl.when(p == 0)
        def _():
            dk_acc[...] = jnp.zeros_like(dk_acc)
            dv_acc[...] = jnp.zeros_like(dv_acc)

    def backward_end(u):
        h, p = u // 3, u % 3
        for d in range(2):

            @pl.when(p == d)
            def _():
                send_ro(d, h).start()
                send_rq(d, h).start()

        @pl.when(p == 2)
        def _():
            kp[h, :KEYS_ROWS, :] = (dk_acc[...] * SCALE).astype(BF16)
            vp[h, :KEYS_ROWS, :] = dv_acc[...].astype(BF16)
            for which in range(2):
                store_kv(which, h).start()

    def events(u):
        @pl.when((u >= 3) & (u <= UNITS) & (u % 3 == 0))
        def _():
            combine(u // 3 - 1)

        @pl.when((u >= LAG + 3) & ((u - LAG) % 3 == 0))
        def _():
            finalize((u - LAG) // 3 - 1)

    def head_step(u, _):
        forward_start(u)
        events(u)
        lax.fori_loop(0, PARTS, lambda c, x: (forward_chunk(u, c), x)[1], 0)
        forward_end(u)
        return 0

    def main_step(u, _):
        forward_start(u)
        events(u)
        backward_start(u - LAG)

        def both(c, x):
            forward_chunk(u, c)
            backward_chunk(u - LAG, c)
            return x

        lax.fori_loop(0, PARTS, both, 0)
        forward_end(u)
        backward_end(u - LAG)
        return 0

    def gate_round(r):
        if r > 0:
            send_gate(r - 1).wait_recv()
            gacc[...] += grecv[r - 1]
        if r < total_rounds:
            gsend[r] = gacc[...]
            send_gate(r).start()

    def tail_step(u, _):
        events(u)
        backward_start(u - LAG)

        def one(c, x):
            backward_chunk(u - LAG, c)
            place = (u - UNITS) * PARTS + c
            for r in range(total_rounds + 1):

                @pl.when(place == 2 * r)
                def _():
                    gate_round(r)

            return x

        lax.fori_loop(0, PARTS, one, 0)
        backward_end(u - LAG)
        return 0

    lax.fori_loop(0, LAG, head_step, 0)
    lax.fori_loop(LAG, UNITS, main_step, 0)
    lax.fori_loop(UNITS, UNITS + LAG, tail_step, 0)
    finalize(KV - 1)
    gsum_ref[...] = gacc[...]

    for r in range(total_rounds):
        send_gate(r).wait_send()
    for h in range(KV):
        for d in range(2):
            send_q(d, h).wait_send()
            send_c(d, h).wait_send()
            send_stat(d, h).wait_send()
            send_lse(d, h).wait_send()
            send_ro(d, h).wait_send()
            send_rq(d, h).wait_send()
            store_kv(d, h).wait()
        store_att(h).wait()
        store_dq(h).wait()


def tail_rows(tile):
    return jnp.pad(tile[KEYS_MAIN:], ((0, KEYS_ROWS - KEYS), (0, 0)))


def shards(ring, rounds, queries, image_keys, image_values, cotangent, gate, tile_list, slot_range):
    position = lax.axis_index("seq")
    keys, values = image_keys[0, 0], image_values[0, 0]
    tanh = jnp.tanh(gate)
    blocks = tile_list.shape[1]
    ranges = slot_range[0].reshape(blocks, BLK, 2)
    block = jnp.arange(blocks)[None, :]
    side = position + jnp.array([-1, 1, 0])[:, None]
    slot = jnp.array([1, 1, 0])[:, None]
    listed = jnp.where(slot == 1, tile_list[0, :, 1][None], tile_list[0, :, 0][None])
    chosen = (block == side) & (listed == position)
    active = (ranges[None, :, :, 0] <= slot[..., None]) & (slot[..., None] < ranges[None, :, :, 1])
    masks = jnp.any(chosen[..., None] & active, axis=1).astype(F32).reshape(3, 1, BLK)

    any_spec = pl.BlockSpec(memory_space=pl.ANY)
    vmem_spec = pl.BlockSpec(memory_space=pltpu.VMEM)
    sems = lambda *shape: pltpu.SemaphoreType.DMA(shape)
    total_rounds = rounds[0] + rounds[1]
    attended, query_grad, key_out, value_out, gate_sum = pl.pallas_call(
        functools.partial(kernel, ring, rounds),
        out_shape=(
            jax.ShapeDtypeStruct((BLK, KV * WIDTH), BF16),
            jax.ShapeDtypeStruct((BLK, KV * WIDTH), BF16),
            jax.ShapeDtypeStruct((KV, KEYS_ROWS, HD), BF16),
            jax.ShapeDtypeStruct((KV, KEYS_ROWS, HD), BF16),
            jax.ShapeDtypeStruct((GROUP, BLK), F32),
        ),
        in_specs=[pl.BlockSpec(memory_space=pltpu.SMEM)] + [vmem_spec] * 3 + [any_spec] * 4,
        out_specs=(any_spec,) * 4 + (vmem_spec,),
        scratch_shapes=[
            pltpu.VMEM((3, KV, BLK, WIDTH), BF16),
            pltpu.VMEM((3, KV, BLK, WIDTH), BF16),
            pltpu.VMEM((KV, KEYS_WIDE, HD), BF16),
            pltpu.VMEM((KV, KEYS_WIDE, HD), BF16),
            pltpu.VMEM((KV, HD, KEYS_WIDE), BF16),
            pltpu.VMEM((KV, HD, KEYS_WIDE), BF16),
            pltpu.VMEM((2, KV, BLK, WIDTH), BF16),
            pltpu.VMEM((2, KV, BLK, WIDTH), BF16),
            pltpu.VMEM((KV, BLK, WIDTH), F32),
            pltpu.VMEM((SLOTS, PARTS, HD, ROWS), F32),
            pltpu.VMEM((SLOTS, PARTS, KEYS_ROWS, ROWS), F32),
            pltpu.VMEM((KEYS_ROWS, HD), F32),
            pltpu.VMEM((KEYS_ROWS, HD), F32),
            pltpu.VMEM((SLOTS, 4, GROUP, BLK), F32),
            pltpu.VMEM((3, KV, 4, GROUP, BLK), F32),
            pltpu.VMEM((2, KV, 4, GROUP, BLK), F32),
            pltpu.VMEM((KV, 2, GROUP, BLK), F32),
            pltpu.VMEM((2, KV, 2, GROUP, BLK), F32),
            pltpu.VMEM((2, GROUP, BLK), F32),
            pltpu.VMEM((GROUP, BLK), F32),
            pltpu.VMEM((total_rounds, GROUP, BLK), F32),
            pltpu.VMEM((total_rounds, GROUP, BLK), F32),
            sems(2, KV),
            sems(2, KV),
            sems(2, 2, KV),
            sems(2, 2, KV),
            sems(2, 2, KV),
            sems(2, 2, KV),
            sems(2, 2, KV),
            sems(2, 2, KV),
            sems(2, KV),
            sems(2, KV),
            sems(2, total_rounds),
        ],
        compiler_params=pltpu.CompilerParams(
            collective_id=0, has_side_effects=True, vmem_limit_bytes=64 * 1024 * 1024 - 65536
        ),
        cost_estimate=pl.CostEstimate(
            flops=2 * 6 * UNITS * 1024 * KEYS * HD,
            bytes_accessed=11_000_000,
            transcendentals=UNITS * 1024 * KEYS,
        ),
    )(
        tanh.reshape(1, 1),
        masks,
        tail_rows(keys),
        tail_rows(values),
        queries[0],
        cotangent[0],
        keys,
        values,
    )

    def tile_of(grad):
        return jnp.transpose(grad[:, :KEYS], (1, 0, 2)).reshape(1, 1, KEYS, KV * HD)

    gate_grad = (1.0 - tanh * tanh) * jnp.sum(gate_sum)
    return attended[None], query_grad[None], tile_of(key_out), tile_of(value_out), gate_grad


def solution(mesh):
    ring = mesh.shape["seq"]
    rounds = (ring.bit_length() - 1, mesh.shape["dp"].bit_length() - 1)
    in_specs = (
        P("dp", "seq", None),
        P("dp", "seq", None, None),
        P("dp", "seq", None, None),
        P("dp", "seq", None),
        P(),
        P("dp", None, None),
        P("dp", None, None),
    )
    out_specs = (
        P("dp", "seq", None),
        P("dp", "seq", None),
        P("dp", "seq", None, None),
        P("dp", "seq", None, None),
        P(),
    )
    return jax.shard_map(
        functools.partial(shards, ring, rounds),
        mesh=mesh,
        in_specs=in_specs,
        out_specs=out_specs,
        check_vma=False,
    )
```

```python
import functools

import jax
import jax.numpy as jnp
from jax import lax
from jax.experimental import pallas as pl
from jax.experimental.pallas import tpu as pltpu
from jax.sharding import PartitionSpec as P

KV = 4
GROUP = 8
HD = 128
BLK = 128
KEYS = 1601
KEYS_MAIN = 1600
KEYS_ROWS = 1616
KEYS_WIDE = 1664
WIDTH = GROUP * HD
HEADS = 4
PARTS = GROUP // HEADS
ROWS = HEADS * BLK
CUTS = tuple((i * 256, min(256, KEYS_ROWS - i * 256)) for i in range(7))
UNITS = 3 * KV
LAG = 4
SLOTS = LAG + 1
LOW = -1e30
SCALE = HD**-0.5
LOG2E = 1.4426950408889634
FACTOR = SCALE * LOG2E
F32 = jnp.float32
BF16 = jnp.bfloat16
MESH = pl.DeviceIdType.MESH


def mm(a, b):
    return jnp.dot(a, b, preferred_element_type=F32)


def pieces(wide):
    return [wide[:, g * BLK : (g + 1) * BLK] for g in range(HEADS)]


def stack_rows(chunk):
    return jnp.concatenate(pieces(chunk), axis=0)


def turn(chunk):
    return jnp.concatenate([piece.T for piece in pieces(chunk)], axis=1)


def slot_tables():
    free, held, fwd, bwd = list(range(SLOTS)), {}, [], []
    for step in range(UNITS + LAG):
        if step < UNITS:
            held[step // 3, (step + 2) % 3] = free.pop(0)
            fwd.append(held[step // 3, (step + 2) % 3])
        if step >= LAG:
            old = step - LAG
            bwd.append(held.pop((old // 3, old % 3)))
            free.append(bwd[-1])
    return fwd, bwd


FWD_SLOT, BWD_SLOT = slot_tables()


def pick(table, index):
    found = jnp.int32(table[0])
    for place, value in enumerate(table[1:], 1):
        found = jnp.where(index == place, value, found)
    return found


def kernel(
    ring,
    rounds,
    gate_ref,
    list_ref,
    range_ref,
    ktail_ref,
    vtail_ref,
    q_hbm,
    cot_hbm,
    k_hbm,
    v_hbm,
    att_hbm,
    dq_hbm,
    dk_hbm,
    dv_hbm,
    gsum_ref,
    mask_ref,
    rmax,
    sbuf,
    qb,
    cb,
    kp,
    vp,
    kt,
    vt,
    ret_o,
    ret_q,
    own_o,
    onum,
    pbuf,
    dk_acc,
    dv_acc,
    stats,
    stats_out,
    stats_in,
    lse_out,
    lse_in,
    cvec,
    dot,
    gacc,
    gsend,
    grecv,
    s_kv,
    s_own,
    s_q,
    s_c,
    s_stat,
    s_lse,
    s_ro,
    s_rq,
    s_out,
    s_kvout,
    s_g,
):
    me = lax.axis_index("seq")
    dpi = lax.axis_index("dp")
    right = lax.rem(me + 1, ring)
    left = lax.rem(me + ring - 1, ring)
    tanh = gate_ref[0, 0]

    def cols(h):
        return pl.ds(pl.multiple_of(h * WIDTH, WIDTH), WIDTH)

    def to_side(d):
        return right if d == 0 else left

    def send_q(d, h):
        return pltpu.make_async_remote_copy(
            src_ref=q_hbm.at[:, cols(h)],
            dst_ref=qb.at[d, h],
            send_sem=s_q.at[0, d, h],
            recv_sem=s_q.at[1, d, h],
            device_id={"seq": to_side(d)},
            device_id_type=MESH,
        )

    def send_c(d, h):
        return pltpu.make_async_remote_copy(
            src_ref=cot_hbm.at[:, cols(h)],
            dst_ref=cb.at[d, h],
            send_sem=s_c.at[0, d, h],
            recv_sem=s_c.at[1, d, h],
            device_id={"seq": to_side(d)},
            device_id_type=MESH,
        )

    def send_stat(p, h):
        return pltpu.make_async_remote_copy(
            src_ref=stats_out.at[p, h],
            dst_ref=stats_in.at[1 - p, h],
            send_sem=s_stat.at[0, p, h],
            recv_sem=s_stat.at[1, 1 - p, h],
            device_id={"seq": to_side(1 - p)},
            device_id_type=MESH,
        )

    def send_lse(d, h):
        return pltpu.make_async_remote_copy(
            src_ref=lse_out.at[h],
            dst_ref=lse_in.at[d, h],
            send_sem=s_lse.at[0, d, h],
            recv_sem=s_lse.at[1, d, h],
            device_id={"seq": to_side(d)},
            device_id_type=MESH,
        )

    def send_ro(p, h):
        return pltpu.make_async_remote_copy(
            src_ref=cb.at[p, h],
            dst_ref=ret_o.at[1 - p, h],
            send_sem=s_ro.at[0, p, h],
            recv_sem=s_ro.at[1, 1 - p, h],
            device_id={"seq": to_side(1 - p)},
            device_id_type=MESH,
        )

    def send_rq(p, h):
        return pltpu.make_async_remote_copy(
            src_ref=qb.at[p, h],
            dst_ref=ret_q.at[1 - p, h],
            send_sem=s_rq.at[0, p, h],
            recv_sem=s_rq.at[1, 1 - p, h],
            device_id={"seq": to_side(1 - p)},
            device_id_type=MESH,
        )

    def gate_partner(r):
        name, place, bit = ("seq", me, r) if r < rounds[0] else ("dp", dpi, r - rounds[0])
        stride = 1 << bit
        return {name: place + stride * (1 - 2 * ((place // stride) % 2))}

    def send_gate(r):
        return pltpu.make_async_remote_copy(
            src_ref=gsend.at[r],
            dst_ref=grecv.at[r],
            send_sem=s_g.at[0, r],
            recv_sem=s_g.at[1, r],
            device_id=gate_partner(r),
            device_id_type=MESH,
        )

    own_q = lambda h: pltpu.make_async_copy(q_hbm.at[:, cols(h)], qb.at[2, h], s_own.at[0, h])
    own_c = lambda h: pltpu.make_async_copy(cot_hbm.at[:, cols(h)], cb.at[2, h], s_own.at[1, h])

    def load_kv(which, h):
        src, dst = ((k_hbm, kp), (v_hbm, vp))[which]
        lanes = pl.ds(pl.multiple_of(h * HD, HD), HD)
        return pltpu.make_async_copy(
            src.at[pl.ds(0, KEYS_MAIN), lanes],
            dst.at[h, pl.ds(0, KEYS_MAIN)],
            s_kv.at[which, h],
        )

    def store_kv(which, h):
        src, dst = ((kp, dk_hbm), (vp, dv_hbm))[which]
        return pltpu.make_async_copy(
            src.at[h, pl.ds(0, KEYS_ROWS)],
            dst.at[:, pl.ds(pl.multiple_of(h * HD, HD), HD)],
            s_kvout.at[which, h],
        )

    def store_att(h):
        return pltpu.make_async_copy(cb.at[2, h], att_hbm.at[:, cols(h)], s_out.at[0, h])

    def store_dq(h):
        return pltpu.make_async_copy(qb.at[2, h], dq_hbm.at[:, cols(h)], s_out.at[1, h])

    for h in range(KV):
        for which in range(2):
            load_kv(which, h).start()
    for h in range(KV):
        own_q(h).start()
        own_c(h).start()

    total_rounds = rounds[0] + rounds[1]
    barrier = pltpu.get_barrier_semaphore()
    for side in (left, right):
        pl.semaphore_signal(barrier, inc=1, device_id={"seq": side}, device_id_type=MESH)
    for r in range(total_rounds):
        pl.semaphore_signal(barrier, inc=1, device_id=gate_partner(r), device_id_type=MESH)
    pl.semaphore_wait(barrier, 2 + total_rounds)

    def send_inputs(h):
        for d in range(2):
            send_q(d, h).start()
        for d in range(2):
            send_c(d, h).start()

    send_inputs(0)
    gacc[...] = jnp.zeros_like(gacc)
    for p, (block, slot) in enumerate(((left, 1), (right, 1), (me, 0))):
        tokens = pl.ds(pl.multiple_of(block * BLK, BLK), BLK)
        first, last = range_ref[0:1, tokens], range_ref[1:2, tokens]
        listed = jnp.where(list_ref[slot, block] == me, 1.0, 0.0).astype(F32)
        mask_ref[p] = jnp.where((first <= slot) & (slot < last), 1.0, 0.0).astype(F32) * listed

    def prepare(h, _):
        for which in range(2):
            load_kv(which, h).wait()
        lanes = pl.ds(pl.multiple_of(h * HD, HD), HD)
        for tail, dst, flipped in ((ktail_ref, kp, kt), (vtail_ref, vp, vt)):
            rows = lax.broadcasted_iota(jnp.int32, (KEYS_ROWS - KEYS_MAIN, HD), 0)
            dst[h, KEYS_MAIN:KEYS_ROWS, :] = jnp.where(
                rows < KEYS - KEYS_MAIN, tail[:, lanes].astype(F32), 0.0
            ).astype(BF16)
            dst[h, KEYS_ROWS:, :] = jnp.zeros((KEYS_WIDE - KEYS_ROWS, HD), BF16)
            for j in range(KEYS_WIDE // HD):
                piece = dst[h, j * HD : (j + 1) * HD, :]
                flipped[h, :, j * HD : (j + 1) * HD] = piece.T
        return 0

    lax.fori_loop(0, KV, prepare, 0)
    send_inputs(1)

    def combine(h):
        send_stat(0, h).wait_recv()
        send_stat(1, h).wait_recv()
        mine = stats_out[2, h]
        low = stats_in[0, h]
        high = stats_in[1, h]
        top = jnp.maximum(jnp.maximum(mine[0], low[0]), high[0])
        shares = [one[1] * jnp.exp2(one[0] - top) for one in (mine, low, high)]
        whole = shares[0] + shares[1] + shares[2]
        some = whole > 0.0
        safe = jnp.where(some, whole, 1.0)
        delta = (shares[0] * mine[2] + shares[1] * low[2] + shares[2] * high[2]) / safe
        gamma = (shares[0] * mine[3] + shares[1] * low[3] + shares[2] * high[3]) / safe
        lse_out[h, 0] = jnp.where(some, top + jnp.log(safe) * LOG2E, 0.0)
        lse_out[h, 1] = jnp.where(some, delta, 0.0)
        gacc[...] += jnp.where(some, gamma, 0.0)
        for d in range(2):
            send_lse(d, h).start()

    def finalize(h):
        for p in range(2):
            send_ro(p, h).wait_recv()
            send_rq(p, h).wait_recv()
        cb[2, h] = (own_o[h] + ret_o[0, h].astype(F32) + ret_o[1, h].astype(F32)).astype(BF16)
        qb[2, h] = (
            qb[2, h].astype(F32) + ret_q[0, h].astype(F32) + ret_q[1, h].astype(F32)
        ).astype(BF16)
        store_att(h).start()
        store_dq(h).start()

    def side_of(u):
        return lax.rem(u + 2, 3)

    def chunk_lanes(c):
        return pl.ds(pl.multiple_of(c * ROWS, ROWS), ROWS)

    def chunk(u, c, scoring, weighing, backing):
        if scoring:
            ahead = jnp.int32(0) if not weighing else jnp.minimum(u * PARTS + c + 1, UNITS * PARTS - 1)
            ua, ca = ahead // PARTS, lax.rem(ahead, PARTS)
            ha, pa = ua // 3, side_of(ua)
            query_ahead = turn(qb[pa, ha, :, chunk_lanes(ca)])
            next_max = None
        if weighing:
            h, p, slot = u // 3, side_of(u), pick(FWD_SLOT, u)
            row_max = rmax[...] * FACTOR
            total = jnp.zeros((1, ROWS), F32)
            out = jnp.zeros((HD, ROWS), F32)
        if backing:
            ub = u - LAG
            hb, pb, slotb = ub // 3, lax.rem(ub, 3), pick(BWD_SLOT, ub)
            lanes = chunk_lanes(c)
            query = stack_rows(qb[pb, hb, :, lanes])
            grad = (tanh * stack_rows(cb[pb, hb, :, lanes]).astype(F32)).astype(BF16)
            grad_t = dot[slotb, c]
            rows = [cvec[i, pl.ds(HEADS * c + g, 1), :] for i in range(2) for g in range(HEADS)]
            weight = jnp.concatenate(rows[:HEADS], axis=1)
            delta = jnp.concatenate(rows[HEADS:], axis=1)
            turned = jnp.zeros((HD, ROWS), F32)
        for start, size in CUTS:
            keys = slice(start, start + size)
            if backing:
                probs = pbuf[slotb, c, keys, :] * weight
                prob_grad = mm(vp[hb, keys, :], grad_t)
                score_grad = (probs * (prob_grad - delta)).astype(BF16)
                dv_acc[keys, :] += mm(probs.astype(BF16), grad)
                dk_acc[keys, :] += mm(score_grad, query)
                turned = turned + mm(kt[hb, :, keys], score_grad)
            if weighing:
                fresh = jnp.exp2(sbuf[keys, :] * FACTOR - row_max)
                pbuf[slot, c, keys, :] = fresh
                total = total + jnp.sum(fresh, axis=0, keepdims=True)
                out = out + mm(vt[h, :, keys], fresh.astype(BF16))
            if scoring:
                scores = mm(kp[ha, keys, :], query_ahead)
                if start + size > KEYS:
                    position = lax.broadcasted_iota(jnp.int32, scores.shape, 0)
                    scores = jnp.where(position < KEYS - start, scores, LOW)
                sbuf[keys, :] = scores
                part = jnp.max(scores, axis=0, keepdims=True)
                next_max = part if next_max is None else jnp.maximum(next_max, part)
        if weighing:
            onum[slot, c] = out
            cot = turn(cb[p, h, :, chunk_lanes(c)].astype(F32))
            fresh_grad = (tanh * cot).astype(BF16)
            dot[slot, c] = fresh_grad
            deltas = jnp.sum(fresh_grad.astype(F32) * out, axis=0, keepdims=True) / total
            gammas = jnp.sum(cot * out, axis=0, keepdims=True) / total
            for kind, row in enumerate((row_max, total, deltas, gammas)):
                for g, piece in enumerate(pieces(row)):
                    stats[slot, kind, pl.ds(HEADS * c + g, 1), :] = piece
        if scoring:
            rmax[...] = next_max
        if backing:
            turned = turned * SCALE
            part = onum[slotb, c] * (weight * tanh)
            part = turn(part)
            qb[pb, hb, :, lanes] = turn(turned).astype(BF16)

            @pl.when(pb < 2)
            def _():
                cb[pb, hb, :, lanes] = part.astype(BF16)

            @pl.when(pb == 2)
            def _():
                own_o[hb, :, lanes] = part

    def forward_start(u):
        h, p = u // 3, side_of(u)

        for d in range(2):

            @pl.when(p == d)
            def _():
                send_q(d, h).wait_recv()
                send_c(d, h).wait_recv()

        for later in range(2, KV):

            @pl.when(u == 3 * later - 5)
            def _():
                send_inputs(later)

        @pl.when(p == 2)
        def _():
            own_q(h).wait()
            own_c(h).wait()

    def forward_end(u):
        h, p, slot = u // 3, side_of(u), pick(FWD_SLOT, u)
        on = mask_ref[p] > 0.0
        for kind, fill in enumerate((LOW, 0.0, 0.0, 0.0)):
            stats_out[p, h, kind] = jnp.where(on, stats[slot, kind], fill)
        for d in range(2):

            @pl.when(p == d)
            def _():
                send_stat(d, h).start()

    def backward_start(u):
        h, p, slot = u // 3, u % 3, pick(BWD_SLOT, u)
        on = mask_ref[p] > 0.0
        for d in range(2):

            @pl.when(p == d)
            def _():
                send_lse(d, h).wait_recv()
                cvec[0] = jnp.where(on, jnp.exp2(stats[slot, 0] - lse_in[d, h, 0]), 0.0)
                cvec[1] = lse_in[d, h, 1]

        @pl.when(p == 2)
        def _():
            cvec[0] = jnp.where(on, jnp.exp2(stats[slot, 0] - lse_out[h, 0]), 0.0)
            cvec[1] = lse_out[h, 1]

        @pl.when(p == 0)
        def _():
            dk_acc[...] = jnp.zeros_like(dk_acc)
            dv_acc[...] = jnp.zeros_like(dv_acc)

    def backward_end(u):
        h, p = u // 3, u % 3
        for d in range(2):

            @pl.when(p == d)
            def _():
                send_ro(d, h).start()
                send_rq(d, h).start()

        @pl.when(p == 2)
        def _():
            kp[h, :KEYS_ROWS, :] = (dk_acc[...] * SCALE).astype(BF16)
            vp[h, :KEYS_ROWS, :] = dv_acc[...].astype(BF16)
            for which in range(2):
                store_kv(which, h).start()

    def chunk_events(u, c):
        @pl.when((u >= 3) & (u <= UNITS) & (u % 3 == 0) & (c == PARTS // 2))
        def _():
            combine(u // 3 - 1)

    def step_events(u):
        @pl.when((u >= 9) & (u % 3 == 0))
        def _():
            finalize(u // 3 - 3)

    def step(u, backing):
        step_events(u)
        if backing:
            backward_start(u - LAG)

        def one(c, x):
            chunk_events(u, c)

            @pl.when((c == PARTS - 1) & (u < UNITS - 1))
            def _():
                forward_start(u + 1)

            chunk(u, c, True, True, backing)
            return x

        lax.fori_loop(0, PARTS, one, 0)
        forward_end(u)
        if backing:
            backward_end(u - LAG)
        return 0

    def gate_round(r):
        if r > 0:
            send_gate(r - 1).wait_recv()
            gacc[...] += grecv[r - 1]
        if r < total_rounds:
            gsend[r] = gacc[...]
            send_gate(r).start()

    def tail_step(u, _):
        step_events(u)
        backward_start(u - LAG)

        def one(c, x):
            chunk_events(u, c)
            chunk(u, c, False, False, True)
            place = (u - UNITS) * PARTS + c
            for r in range(total_rounds):

                @pl.when(place == 1 + r)
                def _():
                    gate_round(r)

            return x

        lax.fori_loop(0, PARTS, one, 0)
        backward_end(u - LAG)
        return 0

    forward_start(jnp.int32(0))
    chunk(0, 0, True, False, False)
    lax.fori_loop(0, LAG, lambda u, x: step(u, False), 0)
    lax.fori_loop(LAG, UNITS, lambda u, x: step(u, True), 0)
    lax.fori_loop(UNITS, UNITS + LAG, tail_step, 0)
    gate_round(total_rounds)
    finalize(KV - 1)
    gsum_ref[0, 0] = (1.0 - tanh * tanh) * jnp.sum(gacc[...])

    for r in range(total_rounds):
        send_gate(r).wait_send()
    for h in range(KV):
        for d in range(2):
            send_q(d, h).wait_send()
            send_c(d, h).wait_send()
            send_stat(d, h).wait_send()
            send_lse(d, h).wait_send()
            send_ro(d, h).wait_send()
            send_rq(d, h).wait_send()
            store_kv(d, h).wait()
        store_att(h).wait()
        store_dq(h).wait()


def shards(ring, rounds, queries, image_keys, image_values, cotangent, gate, tile_list, slot_range):
    keys, values = image_keys[0, 0], image_values[0, 0]
    tanh = jnp.tanh(gate)
    any_spec = pl.BlockSpec(memory_space=pl.ANY)
    smem_spec = pl.BlockSpec(memory_space=pltpu.SMEM)
    tail_rows = KEYS_ROWS - KEYS_MAIN
    tail_spec = pl.BlockSpec((tail_rows, KV * HD), lambda i: (KEYS_MAIN // tail_rows, 0))
    vmem_spec = pl.BlockSpec(memory_space=pltpu.VMEM)
    sems = lambda *shape: pltpu.SemaphoreType.DMA(shape)
    total_rounds = rounds[0] + rounds[1]
    attended, query_grad, key_out, value_out, gate_out = pl.pallas_call(
        functools.partial(kernel, ring, rounds),
        out_shape=(
            jax.ShapeDtypeStruct((BLK, KV * WIDTH), BF16),
            jax.ShapeDtypeStruct((BLK, KV * WIDTH), BF16),
            jax.ShapeDtypeStruct((KEYS_ROWS, KV * HD), BF16),
            jax.ShapeDtypeStruct((KEYS_ROWS, KV * HD), BF16),
            jax.ShapeDtypeStruct((1, 1), F32),
        ),
        grid=(1,),
        in_specs=[smem_spec, smem_spec, vmem_spec, tail_spec, tail_spec] + [any_spec] * 4,
        out_specs=(any_spec,) * 4 + (smem_spec,),
        scratch_shapes=[
            pltpu.VMEM((3, 1, BLK), F32),
            pltpu.VMEM((1, ROWS), F32),
            pltpu.VMEM((KEYS_ROWS, ROWS), F32),
            pltpu.VMEM((3, KV, BLK, WIDTH), BF16),
            pltpu.VMEM((3, KV, BLK, WIDTH), BF16),
            pltpu.VMEM((KV, KEYS_WIDE, HD), BF16),
            pltpu.VMEM((KV, KEYS_WIDE, HD), BF16),
            pltpu.VMEM((KV, HD, KEYS_WIDE), BF16),
            pltpu.VMEM((KV, HD, KEYS_WIDE), BF16),
            pltpu.VMEM((2, KV, BLK, WIDTH), BF16),
            pltpu.VMEM((2, KV, BLK, WIDTH), BF16),
            pltpu.VMEM((KV, BLK, WIDTH), F32),
            pltpu.VMEM((SLOTS, PARTS, HD, ROWS), F32),
            pltpu.VMEM((SLOTS, PARTS, KEYS_ROWS, ROWS), F32),
            pltpu.VMEM((KEYS_ROWS, HD), F32),
            pltpu.VMEM((KEYS_ROWS, HD), F32),
            pltpu.VMEM((SLOTS, 4, GROUP, BLK), F32),
            pltpu.VMEM((3, KV, 4, GROUP, BLK), F32),
            pltpu.VMEM((2, KV, 4, GROUP, BLK), F32),
            pltpu.VMEM((KV, 2, GROUP, BLK), F32),
            pltpu.VMEM((2, KV, 2, GROUP, BLK), F32),
            pltpu.VMEM((2, GROUP, BLK), F32),
            pltpu.VMEM((SLOTS, PARTS, HD, ROWS), BF16),
            pltpu.VMEM((GROUP, BLK), F32),
            pltpu.VMEM((total_rounds, GROUP, BLK), F32),
            pltpu.VMEM((total_rounds, GROUP, BLK), F32),
            sems(2, KV),
            sems(2, KV),
            sems(2, 2, KV),
            sems(2, 2, KV),
            sems(2, 2, KV),
            sems(2, 2, KV),
            sems(2, 2, KV),
            sems(2, 2, KV),
            sems(2, KV),
            sems(2, KV),
            sems(2, total_rounds),
        ],
        compiler_params=pltpu.CompilerParams(
            collective_id=0, has_side_effects=True, vmem_limit_bytes=64 * 1024 * 1024 - 65536
        ),
        cost_estimate=pl.CostEstimate(
            flops=2 * 6 * UNITS * 1024 * KEYS * HD,
            bytes_accessed=11_000_000,
            transcendentals=UNITS * 1024 * KEYS,
        ),
    )(
        tanh.reshape(1, 1),
        tile_list[0].T,
        slot_range[0].T,
        keys,
        values,
        queries[0],
        cotangent[0],
        keys,
        values,
    )

    return (
        attended[None],
        query_grad[None],
        key_out[None, None, :KEYS],
        value_out[None, None, :KEYS],
        gate_out.reshape(()),
    )


def solution(mesh):
    ring = mesh.shape["seq"]
    rounds = (ring.bit_length() - 1, mesh.shape["dp"].bit_length() - 1)
    in_specs = (
        P("dp", "seq", None),
        P("dp", "seq", None, None),
        P("dp", "seq", None, None),
        P("dp", "seq", None),
        P(),
        P("dp", None, None),
        P("dp", None, None),
    )
    out_specs = (
        P("dp", "seq", None),
        P("dp", "seq", None),
        P("dp", "seq", None, None),
        P("dp", "seq", None, None),
        P(),
    )
    return jax.shard_map(
        functools.partial(shards, ring, rounds),
        mesh=mesh,
        in_specs=in_specs,
        out_specs=out_specs,
        check_vma=False,
    )
```

```python
import functools

import jax
import jax.numpy as jnp
from jax import lax
from jax.experimental import pallas as pl
from jax.experimental.pallas import tpu as pltpu
from jax.sharding import PartitionSpec as P

KV = 4
GROUP = 8
HD = 128
BLK = 128
KEYS = 1601
KEYS_MAIN = 1600
KEYS_ROWS = 1616
KEYS_WIDE = 1664
WIDTH = GROUP * HD
HEADS = 4
PARTS = GROUP // HEADS
ROWS = HEADS * BLK
CUTS = tuple((i * 256, min(256, KEYS_ROWS - i * 256)) for i in range(7))
UNITS = 3 * KV
LAG = 4
SLOTS = LAG + 1
FWD_SIDE = (2, 0, 1) * KV
BWD_SIDE = (2, 0, 1) * (KV - 1) + (0, 1, 2)
LOW = -1e30
SCALE = HD**-0.5
LOG2E = 1.4426950408889634
FACTOR = SCALE * LOG2E
F32 = jnp.float32
BF16 = jnp.bfloat16
MESH = pl.DeviceIdType.MESH


def mm(a, b):
    return jnp.dot(a, b, preferred_element_type=F32)


def pieces(wide):
    return [wide[:, g * BLK : (g + 1) * BLK] for g in range(HEADS)]


def stack_rows(chunk):
    return jnp.concatenate(pieces(chunk), axis=0)


def turn(chunk):
    return jnp.concatenate([piece.T for piece in pieces(chunk)], axis=1)


def slot_tables():
    free, held, fwd, bwd = list(range(SLOTS)), {}, [], []
    for step in range(UNITS + LAG):
        if step < UNITS:
            held[step // 3, FWD_SIDE[step]] = free.pop(0)
            fwd.append(held[step // 3, FWD_SIDE[step]])
        if step >= LAG:
            old = step - LAG
            bwd.append(held.pop((old // 3, BWD_SIDE[old])))
            free.append(bwd[-1])
    return fwd, bwd


FWD_SLOT, BWD_SLOT = slot_tables()


def pick(table, index):
    found = jnp.int32(table[0])
    for place, value in enumerate(table[1:], 1):
        found = jnp.where(index == place, value, found)
    return found


def kernel(
    ring,
    rounds,
    gate_ref,
    list_ref,
    range_ref,
    ktail_ref,
    vtail_ref,
    q_hbm,
    cot_hbm,
    k_hbm,
    v_hbm,
    att_hbm,
    dq_hbm,
    dk_hbm,
    dv_hbm,
    gsum_ref,
    mask_ref,
    rmax,
    sbuf,
    qb,
    cb,
    kp,
    vp,
    kt,
    vt,
    ret_o,
    ret_q,
    own_o,
    onum,
    pbuf,
    dk_acc,
    dv_acc,
    stats,
    stats_out,
    stats_in,
    lse_out,
    lse_in,
    cvec,
    dot,
    gacc,
    gsend,
    grecv,
    s_kv,
    s_own,
    s_q,
    s_c,
    s_stat,
    s_lse,
    s_ro,
    s_rq,
    s_out,
    s_kvout,
    s_g,
):
    me = lax.axis_index("seq")
    dpi = lax.axis_index("dp")
    right = lax.rem(me + 1, ring)
    left = lax.rem(me + ring - 1, ring)
    tanh = gate_ref[0, 0]

    def cols(h):
        return pl.ds(pl.multiple_of(h * WIDTH, WIDTH), WIDTH)

    def to_side(d):
        return right if d == 0 else left

    def send_q(d, h):
        return pltpu.make_async_remote_copy(
            src_ref=q_hbm.at[:, cols(h)],
            dst_ref=qb.at[d, h],
            send_sem=s_q.at[0, d, h],
            recv_sem=s_q.at[1, d, h],
            device_id={"seq": to_side(d)},
            device_id_type=MESH,
        )

    def send_c(d, h):
        return pltpu.make_async_remote_copy(
            src_ref=cot_hbm.at[:, cols(h)],
            dst_ref=cb.at[d, h],
            send_sem=s_c.at[0, d, h],
            recv_sem=s_c.at[1, d, h],
            device_id={"seq": to_side(d)},
            device_id_type=MESH,
        )

    def send_stat(p, h):
        return pltpu.make_async_remote_copy(
            src_ref=stats_out.at[p, h],
            dst_ref=stats_in.at[1 - p, h],
            send_sem=s_stat.at[0, p, h],
            recv_sem=s_stat.at[1, 1 - p, h],
            device_id={"seq": to_side(1 - p)},
            device_id_type=MESH,
        )

    def send_lse(d, h):
        return pltpu.make_async_remote_copy(
            src_ref=lse_out.at[h],
            dst_ref=lse_in.at[d, h],
            send_sem=s_lse.at[0, d, h],
            recv_sem=s_lse.at[1, d, h],
            device_id={"seq": to_side(d)},
            device_id_type=MESH,
        )

    def chunk_lanes(c):
        return pl.ds(pl.multiple_of(c * ROWS, ROWS), ROWS)

    def send_ro(p, h, c):
        return pltpu.make_async_remote_copy(
            src_ref=cb.at[p, h, :, chunk_lanes(c)],
            dst_ref=ret_o.at[1 - p, h, :, chunk_lanes(c)],
            send_sem=s_ro.at[0, p, h, c],
            recv_sem=s_ro.at[1, 1 - p, h, c],
            device_id={"seq": to_side(1 - p)},
            device_id_type=MESH,
        )

    def send_rq(p, h, c):
        return pltpu.make_async_remote_copy(
            src_ref=qb.at[p, h, :, chunk_lanes(c)],
            dst_ref=ret_q.at[1 - p, h, :, chunk_lanes(c)],
            send_sem=s_rq.at[0, p, h, c],
            recv_sem=s_rq.at[1, 1 - p, h, c],
            device_id={"seq": to_side(1 - p)},
            device_id_type=MESH,
        )

    def gate_partner(r):
        name, place, bit = ("seq", me, r) if r < rounds[0] else ("dp", dpi, r - rounds[0])
        stride = 1 << bit
        return {name: place + stride * (1 - 2 * ((place // stride) % 2))}

    def send_gate(r):
        return pltpu.make_async_remote_copy(
            src_ref=gsend.at[r],
            dst_ref=grecv.at[r],
            send_sem=s_g.at[0, r],
            recv_sem=s_g.at[1, r],
            device_id=gate_partner(r),
            device_id_type=MESH,
        )

    own_q = lambda h: pltpu.make_async_copy(q_hbm.at[:, cols(h)], qb.at[2, h], s_own.at[0, h])
    own_c = lambda h: pltpu.make_async_copy(cot_hbm.at[:, cols(h)], cb.at[2, h], s_own.at[1, h])

    def load_kv(which, h):
        src, dst = ((k_hbm, kp), (v_hbm, vp))[which]
        lanes = pl.ds(pl.multiple_of(h * HD, HD), HD)
        return pltpu.make_async_copy(
            src.at[pl.ds(0, KEYS_MAIN), lanes],
            dst.at[h, pl.ds(0, KEYS_MAIN)],
            s_kv.at[which, h],
        )

    def store_kv(which, h):
        src, dst = ((kp, dk_hbm), (vp, dv_hbm))[which]
        return pltpu.make_async_copy(
            src.at[h, pl.ds(0, KEYS_ROWS)],
            dst.at[:, pl.ds(pl.multiple_of(h * HD, HD), HD)],
            s_kvout.at[which, h],
        )

    def store_att(h):
        return pltpu.make_async_copy(cb.at[2, h], att_hbm.at[:, cols(h)], s_out.at[0, h])

    def store_dq(h):
        return pltpu.make_async_copy(qb.at[2, h], dq_hbm.at[:, cols(h)], s_out.at[1, h])

    for h in range(KV):
        for which in range(2):
            load_kv(which, h).start()
    for h in range(KV):
        own_q(h).start()
        own_c(h).start()

    total_rounds = rounds[0] + rounds[1]
    barrier = pltpu.get_barrier_semaphore()
    for side in (left, right):
        pl.semaphore_signal(barrier, inc=1, device_id={"seq": side}, device_id_type=MESH)
    for r in range(total_rounds):
        pl.semaphore_signal(barrier, inc=1, device_id=gate_partner(r), device_id_type=MESH)
    pl.semaphore_wait(barrier, 2 + total_rounds)

    def send_inputs(h):
        for d in range(2):
            send_q(d, h).start()
        for d in range(2):
            send_c(d, h).start()

    send_inputs(0)
    gacc[...] = jnp.zeros_like(gacc)
    for p, (block, slot) in enumerate(((left, 1), (right, 1), (me, 0))):
        tokens = pl.ds(pl.multiple_of(block * BLK, BLK), BLK)
        first, last = range_ref[0:1, tokens], range_ref[1:2, tokens]
        listed = jnp.where(list_ref[slot, block] == me, 1.0, 0.0).astype(F32)
        mask_ref[p] = jnp.where((first <= slot) & (slot < last), 1.0, 0.0).astype(F32) * listed

    def prepare(h, _):
        for which in range(2):
            load_kv(which, h).wait()
        lanes = pl.ds(pl.multiple_of(h * HD, HD), HD)
        for tail, dst, flipped in ((ktail_ref, kp, kt), (vtail_ref, vp, vt)):
            rows = lax.broadcasted_iota(jnp.int32, (KEYS_ROWS - KEYS_MAIN, HD), 0)
            dst[h, KEYS_MAIN:KEYS_ROWS, :] = jnp.where(
                rows < KEYS - KEYS_MAIN, tail[:, lanes].astype(F32), 0.0
            ).astype(BF16)
            dst[h, KEYS_ROWS:, :] = jnp.zeros((KEYS_WIDE - KEYS_ROWS, HD), BF16)
            for j in range(KEYS_WIDE // HD):
                piece = dst[h, j * HD : (j + 1) * HD, :]
                flipped[h, :, j * HD : (j + 1) * HD] = piece.T
        return 0

    lax.fori_loop(0, KV, prepare, 0)

    def combine(h):
        send_stat(0, h).wait_recv()
        send_stat(1, h).wait_recv()
        mine = stats_out[2, h]
        low = stats_in[0, h]
        high = stats_in[1, h]
        top = jnp.maximum(jnp.maximum(mine[0], low[0]), high[0])
        shares = [one[1] * jnp.exp2(one[0] - top) for one in (mine, low, high)]
        whole = shares[0] + shares[1] + shares[2]
        some = whole > 0.0
        safe = jnp.where(some, whole, 1.0)
        delta = (shares[0] * mine[2] + shares[1] * low[2] + shares[2] * high[2]) / safe
        gamma = (shares[0] * mine[3] + shares[1] * low[3] + shares[2] * high[3]) / safe
        lse_out[h, 0] = jnp.where(some, top + jnp.log(safe) * LOG2E, 0.0)
        lse_out[h, 1] = jnp.where(some, delta, 0.0)
        gacc[...] += jnp.where(some, gamma, 0.0)
        for d in range(2):
            send_lse(d, h).start()

    def finalize(h):
        for p in range(2):
            for c in range(PARTS):
                send_ro(p, h, c).wait_recv()
                send_rq(p, h, c).wait_recv()
        cb[2, h] = (own_o[h] + ret_o[0, h].astype(F32) + ret_o[1, h].astype(F32)).astype(BF16)
        qb[2, h] = (
            qb[2, h].astype(F32) + ret_q[0, h].astype(F32) + ret_q[1, h].astype(F32)
        ).astype(BF16)
        store_att(h).start()
        store_dq(h).start()

    def side_of(u):
        return lax.rem(u + 2, 3)

    def back_side(u):
        return lax.rem(jnp.where(u < UNITS - 3, u + 2, u), 3)

    def chunk(u, c, scoring, weighing, backing):
        if scoring:
            ahead = jnp.int32(0) if not weighing else jnp.minimum(u * PARTS + c + 1, UNITS * PARTS - 1)
            ua, ca = ahead // PARTS, lax.rem(ahead, PARTS)
            ha, pa = ua // 3, side_of(ua)
            query_ahead = turn(qb[pa, ha, :, chunk_lanes(ca)])
            next_max = None
        if weighing:
            h, p, slot = u // 3, side_of(u), pick(FWD_SLOT, u)
            row_max = rmax[...] * FACTOR
            total = jnp.zeros((1, ROWS), F32)
            out = jnp.zeros((HD, ROWS), F32)
        if backing:
            ub = u - LAG
            hb, pb, slotb = ub // 3, back_side(ub), pick(BWD_SLOT, ub)
            lanes = chunk_lanes(c)
            query = stack_rows(qb[pb, hb, :, lanes])
            grad = (tanh * stack_rows(cb[pb, hb, :, lanes]).astype(F32)).astype(BF16)
            grad_t = dot[slotb, c]
            rows = [cvec[i, pl.ds(HEADS * c + g, 1), :] for i in range(2) for g in range(HEADS)]
            weight = jnp.concatenate(rows[:HEADS], axis=1)
            delta = jnp.concatenate(rows[HEADS:], axis=1)
            turned = jnp.zeros((HD, ROWS), F32)
        for start, size in CUTS:
            keys = slice(start, start + size)
            if backing:
                probs = pbuf[slotb, c, keys, :] * weight
                prob_grad = mm(vp[hb, keys, :], grad_t)
                score_grad = (probs * (prob_grad - delta)).astype(BF16)
                dv_acc[keys, :] += mm(probs.astype(BF16), grad)
                dk_acc[keys, :] += mm(score_grad, query)
                turned = turned + mm(kt[hb, :, keys], score_grad)
            if weighing:
                fresh = jnp.exp2(sbuf[keys, :] * FACTOR - row_max)
                pbuf[slot, c, keys, :] = fresh
                total = total + jnp.sum(fresh, axis=0, keepdims=True)
                out = out + mm(vt[h, :, keys], fresh.astype(BF16))
            if scoring:
                scores = mm(kp[ha, keys, :], query_ahead)
                if start + size > KEYS:
                    position = lax.broadcasted_iota(jnp.int32, scores.shape, 0)
                    scores = jnp.where(position < KEYS - start, scores, LOW)
                sbuf[keys, :] = scores
                part = jnp.max(scores, axis=0, keepdims=True)
                next_max = part if next_max is None else jnp.maximum(next_max, part)
        if weighing:
            onum[slot, c] = out
            cot = turn(cb[p, h, :, chunk_lanes(c)].astype(F32))
            fresh_grad = (tanh * cot).astype(BF16)
            dot[slot, c] = fresh_grad
            deltas = jnp.sum(fresh_grad.astype(F32) * out, axis=0, keepdims=True) / total
            gammas = jnp.sum(cot * out, axis=0, keepdims=True) / total
            for kind, row in enumerate((row_max, total, deltas, gammas)):
                for g, piece in enumerate(pieces(row)):
                    stats[slot, kind, pl.ds(HEADS * c + g, 1), :] = piece
        if scoring:
            rmax[...] = next_max
        if backing:
            turned = turned * SCALE
            part = onum[slotb, c] * (weight * tanh)
            part = turn(part)
            qb[pb, hb, :, lanes] = turn(turned).astype(BF16)

            for d in range(2):

                @pl.when(pb == d)
                def _():
                    cb[d, hb, :, lanes] = part.astype(BF16)
                    send_ro(d, hb, c).start()
                    send_rq(d, hb, c).start()

            @pl.when(pb == 2)
            def _():
                own_o[hb, :, lanes] = part

    def wait_query(u):
        h, p = u // 3, side_of(u)
        for d in range(2):

            @pl.when(p == d)
            def _():
                send_q(d, h).wait_recv()

        @pl.when(p == 2)
        def _():
            own_q(h).wait()

        @pl.when(u == 1)
        def _():
            for d in range(2):
                send_q(d, 1).start()

    def wait_cotangent(u):
        h, p = u // 3, side_of(u)
        for d in range(2):

            @pl.when(p == d)
            def _():
                send_c(d, h).wait_recv()

        @pl.when(p == 2)
        def _():
            own_c(h).wait()

        @pl.when(u == 1)
        def _():
            for d in range(2):
                send_c(d, 1).start()

        for later, place in ((2, 2), (3, 4)):

            @pl.when(u == place)
            def _():
                send_inputs(later)

    def forward_end(u):
        h, p, slot = u // 3, side_of(u), pick(FWD_SLOT, u)
        on = mask_ref[p] > 0.0
        for kind, fill in enumerate((LOW, 0.0, 0.0, 0.0)):
            stats_out[p, h, kind] = jnp.where(on, stats[slot, kind], fill)
        for d in range(2):

            @pl.when(p == d)
            def _():
                send_stat(d, h).start()

    def backward_start(u):
        h, p, slot = u // 3, back_side(u), pick(BWD_SLOT, u)
        on = mask_ref[p] > 0.0
        for d in range(2):

            @pl.when(p == d)
            def _():
                send_lse(d, h).wait_recv()
                cvec[0] = jnp.where(on, jnp.exp2(stats[slot, 0] - lse_in[d, h, 0]), 0.0)
                cvec[1] = lse_in[d, h, 1]

        @pl.when(p == 2)
        def _():
            cvec[0] = jnp.where(on, jnp.exp2(stats[slot, 0] - lse_out[h, 0]), 0.0)
            cvec[1] = lse_out[h, 1]

        @pl.when(lax.rem(u, 3) == 0)
        def _():
            dk_acc[...] = jnp.zeros_like(dk_acc)
            dv_acc[...] = jnp.zeros_like(dv_acc)

    def backward_end(u):
        h = u // 3

        @pl.when(lax.rem(u, 3) == 2)
        def _():
            kp[h, :KEYS_ROWS, :] = (dk_acc[...] * SCALE).astype(BF16)
            vp[h, :KEYS_ROWS, :] = dv_acc[...].astype(BF16)
            for which in range(2):
                store_kv(which, h).start()

    def chunk_events(u, c):
        @pl.when((u >= 3) & (u <= UNITS) & (u % 3 == 0) & (c == PARTS // 2))
        def _():
            combine(u // 3 - 1)

    def step_events(u):
        @pl.when((u >= 9) & (u % 3 == 0))
        def _():
            finalize(u // 3 - 3)

    def step(u, backing):
        step_events(u)
        wait_cotangent(u)
        if backing:
            backward_start(u - LAG)

        def one(c, x):
            chunk_events(u, c)

            @pl.when((c == PARTS - 1) & (u < UNITS - 1))
            def _():
                wait_query(u + 1)

            chunk(u, c, True, True, backing)
            return x

        lax.fori_loop(0, PARTS, one, 0)
        forward_end(u)
        if backing:
            backward_end(u - LAG)
        return 0

    def gate_round(r):
        if r > 0:
            send_gate(r - 1).wait_recv()
            gacc[...] += grecv[r - 1]
        if r < total_rounds:
            gsend[r] = gacc[...]
            send_gate(r).start()

    def tail_step(u, _):
        step_events(u)
        backward_start(u - LAG)

        def one(c, x):
            chunk_events(u, c)
            chunk(u, c, False, False, True)
            place = (u - UNITS) * PARTS + c
            for r in range(total_rounds):

                @pl.when(place == 1 + r)
                def _():
                    gate_round(r)

            return x

        lax.fori_loop(0, PARTS, one, 0)
        backward_end(u - LAG)
        return 0

    wait_query(jnp.int32(0))
    chunk(0, 0, True, False, False)
    lax.fori_loop(0, LAG, lambda u, x: step(u, False), 0)
    lax.fori_loop(LAG, UNITS, lambda u, x: step(u, True), 0)
    lax.fori_loop(UNITS, UNITS + LAG, tail_step, 0)
    gate_round(total_rounds)
    finalize(KV - 1)
    gsum_ref[0, 0] = (1.0 - tanh * tanh) * jnp.sum(gacc[...])

    for r in range(total_rounds):
        send_gate(r).wait_send()
    for h in range(KV):
        for d in range(2):
            send_q(d, h).wait_send()
            send_c(d, h).wait_send()
            send_stat(d, h).wait_send()
            send_lse(d, h).wait_send()
            for c in range(PARTS):
                send_ro(d, h, c).wait_send()
                send_rq(d, h, c).wait_send()
            store_kv(d, h).wait()
        store_att(h).wait()
        store_dq(h).wait()


def shards(ring, rounds, queries, image_keys, image_values, cotangent, gate, tile_list, slot_range):
    keys, values = image_keys[0, 0], image_values[0, 0]
    tanh = jnp.tanh(gate)
    any_spec = pl.BlockSpec(memory_space=pl.ANY)
    smem_spec = pl.BlockSpec(memory_space=pltpu.SMEM)
    tail_rows = KEYS_ROWS - KEYS_MAIN
    tail_spec = pl.BlockSpec((tail_rows, KV * HD), lambda i: (KEYS_MAIN // tail_rows, 0))
    vmem_spec = pl.BlockSpec(memory_space=pltpu.VMEM)
    sems = lambda *shape: pltpu.SemaphoreType.DMA(shape)
    total_rounds = rounds[0] + rounds[1]
    attended, query_grad, key_out, value_out, gate_out = pl.pallas_call(
        functools.partial(kernel, ring, rounds),
        out_shape=(
            jax.ShapeDtypeStruct((BLK, KV * WIDTH), BF16),
            jax.ShapeDtypeStruct((BLK, KV * WIDTH), BF16),
            jax.ShapeDtypeStruct((KEYS_ROWS, KV * HD), BF16),
            jax.ShapeDtypeStruct((KEYS_ROWS, KV * HD), BF16),
            jax.ShapeDtypeStruct((1, 1), F32),
        ),
        grid=(1,),
        in_specs=[smem_spec, smem_spec, vmem_spec, tail_spec, tail_spec] + [any_spec] * 4,
        out_specs=(any_spec,) * 4 + (smem_spec,),
        scratch_shapes=[
            pltpu.VMEM((3, 1, BLK), F32),
            pltpu.VMEM((1, ROWS), F32),
            pltpu.VMEM((KEYS_ROWS, ROWS), F32),
            pltpu.VMEM((3, KV, BLK, WIDTH), BF16),
            pltpu.VMEM((3, KV, BLK, WIDTH), BF16),
            pltpu.VMEM((KV, KEYS_WIDE, HD), BF16),
            pltpu.VMEM((KV, KEYS_WIDE, HD), BF16),
            pltpu.VMEM((KV, HD, KEYS_WIDE), BF16),
            pltpu.VMEM((KV, HD, KEYS_WIDE), BF16),
            pltpu.VMEM((2, KV, BLK, WIDTH), BF16),
            pltpu.VMEM((2, KV, BLK, WIDTH), BF16),
            pltpu.VMEM((KV, BLK, WIDTH), F32),
            pltpu.VMEM((SLOTS, PARTS, HD, ROWS), F32),
            pltpu.VMEM((SLOTS, PARTS, KEYS_ROWS, ROWS), F32),
            pltpu.VMEM((KEYS_ROWS, HD), F32),
            pltpu.VMEM((KEYS_ROWS, HD), F32),
            pltpu.VMEM((SLOTS, 4, GROUP, BLK), F32),
            pltpu.VMEM((3, KV, 4, GROUP, BLK), F32),
            pltpu.VMEM((2, KV, 4, GROUP, BLK), F32),
            pltpu.VMEM((KV, 2, GROUP, BLK), F32),
            pltpu.VMEM((2, KV, 2, GROUP, BLK), F32),
            pltpu.VMEM((2, GROUP, BLK), F32),
            pltpu.VMEM((SLOTS, PARTS, HD, ROWS), BF16),
            pltpu.VMEM((GROUP, BLK), F32),
            pltpu.VMEM((total_rounds, GROUP, BLK), F32),
            pltpu.VMEM((total_rounds, GROUP, BLK), F32),
            sems(2, KV),
            sems(2, KV),
            sems(2, 2, KV),
            sems(2, 2, KV),
            sems(2, 2, KV),
            sems(2, 2, KV),
            sems(2, 2, KV, PARTS),
            sems(2, 2, KV, PARTS),
            sems(2, KV),
            sems(2, KV),
            sems(2, total_rounds),
        ],
        compiler_params=pltpu.CompilerParams(
            collective_id=0, has_side_effects=True, vmem_limit_bytes=64 * 1024 * 1024 - 65536
        ),
        cost_estimate=pl.CostEstimate(
            flops=2 * 6 * UNITS * 1024 * KEYS * HD,
            bytes_accessed=11_000_000,
            transcendentals=UNITS * 1024 * KEYS,
        ),
    )(
        tanh.reshape(1, 1),
        tile_list[0].T,
        slot_range[0].T,
        keys,
        values,
        queries[0],
        cotangent[0],
        keys,
        values,
    )

    return (
        attended[None],
        query_grad[None],
        key_out[None, None, :KEYS],
        value_out[None, None, :KEYS],
        gate_out.reshape(()),
    )


def solution(mesh):
    ring = mesh.shape["seq"]
    rounds = (ring.bit_length() - 1, mesh.shape["dp"].bit_length() - 1)
    in_specs = (
        P("dp", "seq", None),
        P("dp", "seq", None, None),
        P("dp", "seq", None, None),
        P("dp", "seq", None),
        P(),
        P("dp", None, None),
        P("dp", None, None),
    )
    out_specs = (
        P("dp", "seq", None),
        P("dp", "seq", None),
        P("dp", "seq", None, None),
        P("dp", "seq", None, None),
        P(),
    )
    return jax.shard_map(
        functools.partial(shards, ring, rounds),
        mesh=mesh,
        in_specs=in_specs,
        out_specs=out_specs,
        check_vma=False,
    )
```

```python
import functools

import jax
import jax.numpy as jnp
from jax import lax
from jax.experimental import pallas as pl
from jax.experimental.pallas import tpu as pltpu
from jax.sharding import PartitionSpec as P

KV = 4
GROUP = 8
HD = 128
BLK = 128
KEYS = 1601
KEYS_MAIN = 1600
KEYS_ROWS = 1616
KEYS_WIDE = 1664
WIDTH = GROUP * HD
HEADS = 4
PARTS = GROUP // HEADS
ROWS = HEADS * BLK
CUTS = ((0, 768), (768, 848))
UNITS = 3 * KV
LAG = 4
SLOTS = LAG + 1
FWD_SIDE = (2, 0, 1) * KV
BWD_SIDE = (2, 0, 1) * (KV - 1) + (0, 1, 2)
LOW = -1e30
VMEM_LIMIT = 64 * 1024 * 1024 - 65536
SCALE = HD**-0.5
LOG2E = 1.4426950408889634
FACTOR = SCALE * LOG2E
F32 = jnp.float32
BF16 = jnp.bfloat16
MESH = pl.DeviceIdType.MESH


def mm(a, b):
    return jnp.dot(a, b, preferred_element_type=F32)


def pieces(wide):
    return [wide[:, g * BLK : (g + 1) * BLK] for g in range(HEADS)]


def stack_rows(chunk):
    return jnp.concatenate(pieces(chunk), axis=0)


def turn(chunk):
    return jnp.concatenate([piece.T for piece in pieces(chunk)], axis=1)


def slot_tables():
    free, held, fwd, bwd = list(range(SLOTS)), {}, [], []
    for step in range(UNITS + LAG):
        if step < UNITS:
            held[step // 3, FWD_SIDE[step]] = free.pop(0)
            fwd.append(held[step // 3, FWD_SIDE[step]])
        if step >= LAG:
            old = step - LAG
            bwd.append(held.pop((old // 3, BWD_SIDE[old])))
            free.append(bwd[-1])
    return fwd, bwd


FWD_SLOT, BWD_SLOT = slot_tables()


def pick(table, index):
    found = jnp.int32(table[0])
    for place, value in enumerate(table[1:], 1):
        found = jnp.where(index == place, value, found)
    return found


def kernel(
    ring,
    rounds,
    gate_ref,
    list_ref,
    range_ref,
    ktail_ref,
    vtail_ref,
    q_hbm,
    cot_hbm,
    k_hbm,
    v_hbm,
    att_hbm,
    dq_hbm,
    dk_hbm,
    dv_hbm,
    gsum_ref,
    mask_ref,
    rmax,
    sbuf,
    qb,
    cb,
    kp,
    vp,
    kt,
    vt,
    ret_o,
    ret_q,
    own_o,
    onum,
    pbuf,
    dk_acc,
    dv_acc,
    stats,
    stats_out,
    stats_in,
    lse_out,
    lse_in,
    cvec,
    dot,
    gacc,
    gsend,
    grecv,
    s_kv,
    s_own,
    s_q,
    s_c,
    s_stat,
    s_lse,
    s_ro,
    s_rq,
    s_out,
    s_kvout,
    s_g,
):
    me = lax.axis_index("seq")
    dpi = lax.axis_index("dp")
    right = lax.rem(me + 1, ring)
    left = lax.rem(me + ring - 1, ring)
    tanh = gate_ref[0, 0]

    def cols(h):
        return pl.ds(pl.multiple_of(h * WIDTH, WIDTH), WIDTH)

    def to_side(d):
        return right if d == 0 else left

    def send_q(d, h):
        return pltpu.make_async_remote_copy(
            src_ref=q_hbm.at[:, cols(h)],
            dst_ref=qb.at[d, h],
            send_sem=s_q.at[0, d, h],
            recv_sem=s_q.at[1, d, h],
            device_id={"seq": to_side(d)},
            device_id_type=MESH,
        )

    def send_c(d, h):
        return pltpu.make_async_remote_copy(
            src_ref=cot_hbm.at[:, cols(h)],
            dst_ref=cb.at[d, h],
            send_sem=s_c.at[0, d, h],
            recv_sem=s_c.at[1, d, h],
            device_id={"seq": to_side(d)},
            device_id_type=MESH,
        )

    def send_stat(p, h):
        return pltpu.make_async_remote_copy(
            src_ref=stats_out.at[p, h],
            dst_ref=stats_in.at[1 - p, h],
            send_sem=s_stat.at[0, p, h],
            recv_sem=s_stat.at[1, 1 - p, h],
            device_id={"seq": to_side(1 - p)},
            device_id_type=MESH,
        )

    def send_lse(d, h):
        return pltpu.make_async_remote_copy(
            src_ref=lse_out.at[h],
            dst_ref=lse_in.at[d, h],
            send_sem=s_lse.at[0, d, h],
            recv_sem=s_lse.at[1, d, h],
            device_id={"seq": to_side(d)},
            device_id_type=MESH,
        )

    def chunk_lanes(c):
        return pl.ds(pl.multiple_of(c * ROWS, ROWS), ROWS)

    def send_ro(p, h, c):
        return pltpu.make_async_remote_copy(
            src_ref=cb.at[p, h, :, chunk_lanes(c)],
            dst_ref=ret_o.at[1 - p, h, :, chunk_lanes(c)],
            send_sem=s_ro.at[0, p, h, c],
            recv_sem=s_ro.at[1, 1 - p, h, c],
            device_id={"seq": to_side(1 - p)},
            device_id_type=MESH,
        )

    def send_rq(p, h, c):
        return pltpu.make_async_remote_copy(
            src_ref=qb.at[p, h, :, chunk_lanes(c)],
            dst_ref=ret_q.at[1 - p, h, :, chunk_lanes(c)],
            send_sem=s_rq.at[0, p, h, c],
            recv_sem=s_rq.at[1, 1 - p, h, c],
            device_id={"seq": to_side(1 - p)},
            device_id_type=MESH,
        )

    def gate_partner(r):
        name, place, bit = ("seq", me, r) if r < rounds[0] else ("dp", dpi, r - rounds[0])
        stride = 1 << bit
        return {name: place + stride * (1 - 2 * ((place // stride) % 2))}

    def send_gate(r):
        return pltpu.make_async_remote_copy(
            src_ref=gsend.at[r],
            dst_ref=grecv.at[r],
            send_sem=s_g.at[0, r],
            recv_sem=s_g.at[1, r],
            device_id=gate_partner(r),
            device_id_type=MESH,
        )

    own_q = lambda h: pltpu.make_async_copy(q_hbm.at[:, cols(h)], qb.at[2, h], s_own.at[0, h])
    own_c = lambda h: pltpu.make_async_copy(cot_hbm.at[:, cols(h)], cb.at[2, h], s_own.at[1, h])

    def load_kv(which, h):
        src, dst = ((k_hbm, kp), (v_hbm, vp))[which]
        lanes = pl.ds(pl.multiple_of(h * HD, HD), HD)
        return pltpu.make_async_copy(
            src.at[pl.ds(0, KEYS_MAIN), lanes],
            dst.at[h, pl.ds(0, KEYS_MAIN)],
            s_kv.at[which, h],
        )

    def store_kv(which, h):
        src, dst = ((kp, dk_hbm), (vp, dv_hbm))[which]
        return pltpu.make_async_copy(
            src.at[h, pl.ds(0, KEYS_ROWS)],
            dst.at[:, pl.ds(pl.multiple_of(h * HD, HD), HD)],
            s_kvout.at[which, h],
        )

    def store_att(h):
        return pltpu.make_async_copy(cb.at[2, h], att_hbm.at[:, cols(h)], s_out.at[0, h])

    def store_dq(h):
        return pltpu.make_async_copy(qb.at[2, h], dq_hbm.at[:, cols(h)], s_out.at[1, h])

    for h in range(KV):
        for which in range(2):
            load_kv(which, h).start()
    for h in range(KV):
        own_q(h).start()
        own_c(h).start()

    total_rounds = rounds[0] + rounds[1]
    barrier = pltpu.get_barrier_semaphore()
    for side in (left, right):
        pl.semaphore_signal(barrier, inc=1, device_id={"seq": side}, device_id_type=MESH)
    for r in range(total_rounds):
        pl.semaphore_signal(barrier, inc=1, device_id=gate_partner(r), device_id_type=MESH)
    pl.semaphore_wait(barrier, 2 + total_rounds)

    def send_inputs(h):
        for d in range(2):
            send_q(d, h).start()
        for d in range(2):
            send_c(d, h).start()

    send_inputs(0)
    gacc[...] = jnp.zeros_like(gacc)
    for p, (block, slot) in enumerate(((left, 1), (right, 1), (me, 0))):
        tokens = pl.ds(pl.multiple_of(block * BLK, BLK), BLK)
        first, last = range_ref[0:1, tokens], range_ref[1:2, tokens]
        listed = jnp.where(list_ref[slot, block] == me, 1.0, 0.0).astype(F32)
        mask_ref[p] = jnp.where((first <= slot) & (slot < last), 1.0, 0.0).astype(F32) * listed

    def prepare(h, _):
        for which in range(2):
            load_kv(which, h).wait()
        lanes = pl.ds(pl.multiple_of(h * HD, HD), HD)
        for tail, dst, flipped in ((ktail_ref, kp, kt), (vtail_ref, vp, vt)):
            rows = lax.broadcasted_iota(jnp.int32, (KEYS_ROWS - KEYS_MAIN, HD), 0)
            dst[h, KEYS_MAIN:KEYS_ROWS, :] = jnp.where(
                rows < KEYS - KEYS_MAIN, tail[:, lanes].astype(F32), 0.0
            ).astype(BF16)
            dst[h, KEYS_ROWS:, :] = jnp.zeros((KEYS_WIDE - KEYS_ROWS, HD), BF16)
            for j in range(KEYS_WIDE // HD):
                piece = dst[h, j * HD : (j + 1) * HD, :]
                flipped[h, :, j * HD : (j + 1) * HD] = piece.T
        return 0

    lax.fori_loop(0, KV, prepare, 0)

    def combine(h):
        send_stat(0, h).wait_recv()
        send_stat(1, h).wait_recv()
        mine = stats_out[2, h]
        low = stats_in[0, h]
        high = stats_in[1, h]
        top = jnp.maximum(jnp.maximum(mine[0], low[0]), high[0])
        shares = [one[1] * jnp.exp2(one[0] - top) for one in (mine, low, high)]
        whole = shares[0] + shares[1] + shares[2]
        some = whole > 0.0
        safe = jnp.where(some, whole, 1.0)
        delta = (shares[0] * mine[2] + shares[1] * low[2] + shares[2] * high[2]) / safe
        gamma = (shares[0] * mine[3] + shares[1] * low[3] + shares[2] * high[3]) / safe
        lse_out[h, 0] = jnp.where(some, top + jnp.log(safe) * LOG2E, 0.0)
        lse_out[h, 1] = jnp.where(some, delta, 0.0)
        gacc[...] += jnp.where(some, gamma, 0.0)
        for d in range(2):
            send_lse(d, h).start()

    def finalize(h):
        for p in range(2):
            for c in range(PARTS):
                send_ro(p, h, c).wait_recv()
                send_rq(p, h, c).wait_recv()
        cb[2, h] = (own_o[h] + ret_o[0, h].astype(F32) + ret_o[1, h].astype(F32)).astype(BF16)
        qb[2, h] = (
            qb[2, h].astype(F32) + ret_q[0, h].astype(F32) + ret_q[1, h].astype(F32)
        ).astype(BF16)
        store_att(h).start()
        store_dq(h).start()

    def side_of(u):
        return lax.rem(u + 2, 3)

    def back_side(u):
        return lax.rem(jnp.where(u < UNITS - 3, u + 2, u), 3)

    def chunk(u, c, scoring, weighing, backing):
        if scoring:
            ahead = jnp.int32(0) if not weighing else jnp.minimum(u * PARTS + c + 1, UNITS * PARTS - 1)
            ua, ca = ahead // PARTS, lax.rem(ahead, PARTS)
            ha, pa = ua // 3, side_of(ua)
            query_ahead = turn(qb[pa, ha, :, chunk_lanes(ca)])
            next_max = None
        if weighing:
            h, p, slot = u // 3, side_of(u), pick(FWD_SLOT, u)
            row_max = rmax[...] * FACTOR
            total = jnp.zeros((1, ROWS), F32)
            out = jnp.zeros((HD, ROWS), F32)
        if backing:
            ub = u - LAG
            hb, pb, slotb = ub // 3, back_side(ub), pick(BWD_SLOT, ub)
            lanes = chunk_lanes(c)
            query = stack_rows(qb[pb, hb, :, lanes])
            grad = (tanh * stack_rows(cb[pb, hb, :, lanes]).astype(F32)).astype(BF16)
            grad_t = dot[slotb, c]
            rows = [cvec[i, pl.ds(HEADS * c + g, 1), :] for i in range(2) for g in range(HEADS)]
            weight = jnp.concatenate(rows[:HEADS], axis=1)
            delta = jnp.concatenate(rows[HEADS:], axis=1)
            turned = jnp.zeros((HD, ROWS), F32)
        for start, size in CUTS:
            keys = slice(start, start + size)
            if backing:
                probs = pbuf[slotb, c, keys, :] * weight
                prob_grad = mm(vp[hb, keys, :], grad_t)
                score_grad = (probs * (prob_grad - delta)).astype(BF16)
                dv_acc[keys, :] += mm(probs.astype(BF16), grad)
                dk_acc[keys, :] += mm(score_grad, query)
                turned = turned + mm(kt[hb, :, keys], score_grad)
            if weighing:
                fresh = jnp.exp2(sbuf[keys, :] * FACTOR - row_max)
                pbuf[slot, c, keys, :] = fresh
                total = total + jnp.sum(fresh, axis=0, keepdims=True)
                out = out + mm(vt[h, :, keys], fresh.astype(BF16))
            if scoring:
                scores = mm(kp[ha, keys, :], query_ahead)
                if start + size > KEYS:
                    position = lax.broadcasted_iota(jnp.int32, scores.shape, 0)
                    scores = jnp.where(position < KEYS - start, scores, LOW)
                sbuf[keys, :] = scores
                part = jnp.max(scores, axis=0, keepdims=True)
                next_max = part if next_max is None else jnp.maximum(next_max, part)
        if weighing:
            onum[slot, c] = out
            cot = turn(cb[p, h, :, chunk_lanes(c)].astype(F32))
            fresh_grad = (tanh * cot).astype(BF16)
            dot[slot, c] = fresh_grad
            deltas = jnp.sum(fresh_grad.astype(F32) * out, axis=0, keepdims=True) / total
            gammas = jnp.sum(cot * out, axis=0, keepdims=True) / total
            for kind, row in enumerate((row_max, total, deltas, gammas)):
                for g, piece in enumerate(pieces(row)):
                    stats[slot, kind, pl.ds(HEADS * c + g, 1), :] = piece
        if scoring:
            rmax[...] = next_max
        if backing:
            turned = turned * SCALE
            part = onum[slotb, c] * (weight * tanh)
            part = turn(part)
            qb[pb, hb, :, lanes] = turn(turned).astype(BF16)

            for d in range(2):

                @pl.when(pb == d)
                def _():
                    cb[d, hb, :, lanes] = part.astype(BF16)
                    send_ro(d, hb, c).start()
                    send_rq(d, hb, c).start()

            @pl.when(pb == 2)
            def _():
                own_o[hb, :, lanes] = part

    def wait_query(u):
        h, p = u // 3, side_of(u)
        for d in range(2):

            @pl.when(p == d)
            def _():
                send_q(d, h).wait_recv()

        @pl.when(p == 2)
        def _():
            own_q(h).wait()

        @pl.when(u == 1)
        def _():
            for d in range(2):
                send_q(d, 1).start()

    def wait_cotangent(u):
        h, p = u // 3, side_of(u)
        for d in range(2):

            @pl.when(p == d)
            def _():
                send_c(d, h).wait_recv()

        @pl.when(p == 2)
        def _():
            own_c(h).wait()

        @pl.when(u == 1)
        def _():
            for d in range(2):
                send_c(d, 1).start()

        for later, place in ((2, 2), (3, 4)):

            @pl.when(u == place)
            def _():
                send_inputs(later)

    def forward_end(u):
        h, p, slot = u // 3, side_of(u), pick(FWD_SLOT, u)
        on = mask_ref[p] > 0.0
        for kind, fill in enumerate((LOW, 0.0, 0.0, 0.0)):
            stats_out[p, h, kind] = jnp.where(on, stats[slot, kind], fill)
        for d in range(2):

            @pl.when(p == d)
            def _():
                send_stat(d, h).start()

    def backward_start(u):
        h, p, slot = u // 3, back_side(u), pick(BWD_SLOT, u)
        on = mask_ref[p] > 0.0
        for d in range(2):

            @pl.when(p == d)
            def _():
                send_lse(d, h).wait_recv()
                cvec[0] = jnp.where(on, jnp.exp2(stats[slot, 0] - lse_in[d, h, 0]), 0.0)
                cvec[1] = lse_in[d, h, 1]

        @pl.when(p == 2)
        def _():
            cvec[0] = jnp.where(on, jnp.exp2(stats[slot, 0] - lse_out[h, 0]), 0.0)
            cvec[1] = lse_out[h, 1]

        @pl.when(lax.rem(u, 3) == 0)
        def _():
            dk_acc[...] = jnp.zeros_like(dk_acc)
            dv_acc[...] = jnp.zeros_like(dv_acc)

    def backward_end(u):
        h = u // 3

        @pl.when(lax.rem(u, 3) == 2)
        def _():
            kp[h, :KEYS_ROWS, :] = (dk_acc[...] * SCALE).astype(BF16)
            vp[h, :KEYS_ROWS, :] = dv_acc[...].astype(BF16)
            for which in range(2):
                store_kv(which, h).start()

    def chunk_events(u, c):
        @pl.when((u >= 3) & (u <= UNITS) & (u % 3 == 0) & (c == PARTS // 2))
        def _():
            combine(u // 3 - 1)

    def step_events(u):
        @pl.when((u >= 9) & (u % 3 == 0))
        def _():
            finalize(u // 3 - 3)

    def step(u, backing):
        step_events(u)
        wait_cotangent(u)
        if backing:
            backward_start(u - LAG)

        def one(c, x):
            chunk_events(u, c)

            @pl.when((c == PARTS - 1) & (u < UNITS - 1))
            def _():
                wait_query(u + 1)

            chunk(u, c, True, True, backing)
            return x

        lax.fori_loop(0, PARTS, one, 0)
        forward_end(u)
        if backing:
            backward_end(u - LAG)
        return 0

    def gate_round(r):
        if r > 0:
            send_gate(r - 1).wait_recv()
            gacc[...] += grecv[r - 1]
        if r < total_rounds:
            gsend[r] = gacc[...]
            send_gate(r).start()

    def tail_step(u, _):
        step_events(u)
        backward_start(u - LAG)

        def one(c, x):
            chunk_events(u, c)
            chunk(u, c, False, False, True)
            place = (u - UNITS) * PARTS + c
            for r in range(total_rounds):

                @pl.when(place == 1 + r)
                def _():
                    gate_round(r)

            return x

        lax.fori_loop(0, PARTS, one, 0)
        backward_end(u - LAG)
        return 0

    wait_query(jnp.int32(0))
    chunk(0, 0, True, False, False)
    lax.fori_loop(0, LAG, lambda u, x: step(u, False), 0)
    lax.fori_loop(LAG, UNITS, lambda u, x: step(u, True), 0)
    lax.fori_loop(UNITS, UNITS + LAG, tail_step, 0)
    gate_round(total_rounds)
    finalize(KV - 1)
    gsum_ref[0, 0] = (1.0 - tanh * tanh) * jnp.sum(gacc[...])

    for r in range(total_rounds):
        send_gate(r).wait_send()
    for h in range(KV):
        for d in range(2):
            send_q(d, h).wait_send()
            send_c(d, h).wait_send()
            send_stat(d, h).wait_send()
            send_lse(d, h).wait_send()
            for c in range(PARTS):
                send_ro(d, h, c).wait_send()
                send_rq(d, h, c).wait_send()
            store_kv(d, h).wait()
        store_att(h).wait()
        store_dq(h).wait()


def hand_on(*refs):
    count = len(refs) // 2
    for source, target in zip(refs[:count], refs[count:]):
        target[...] = source[...]


def shards(ring, rounds, queries, image_keys, image_values, cotangent, gate, tile_list, slot_range):
    keys, values = image_keys[0, 0], image_values[0, 0]
    tanh = jnp.tanh(gate)
    any_spec = pl.BlockSpec(memory_space=pl.ANY)
    smem_spec = pl.BlockSpec(memory_space=pltpu.SMEM)
    tail_rows = KEYS_ROWS - KEYS_MAIN
    tail_spec = pl.BlockSpec((tail_rows, KV * HD), lambda i: (KEYS_MAIN // tail_rows, 0))
    vmem_spec = pl.BlockSpec(memory_space=pltpu.VMEM)
    sems = lambda *shape: pltpu.SemaphoreType.DMA(shape)
    total_rounds = rounds[0] + rounds[1]
    attended, query_grad, key_out, value_out, gate_out = pl.pallas_call(
        functools.partial(kernel, ring, rounds),
        out_shape=(
            jax.ShapeDtypeStruct((BLK, KV * WIDTH), BF16),
            jax.ShapeDtypeStruct((BLK, KV * WIDTH), BF16),
            jax.ShapeDtypeStruct((KEYS_ROWS, KV * HD), BF16),
            jax.ShapeDtypeStruct((KEYS_ROWS, KV * HD), BF16),
            jax.ShapeDtypeStruct((1, 1), F32),
        ),
        grid=(1,),
        in_specs=[smem_spec, smem_spec, vmem_spec, tail_spec, tail_spec] + [any_spec] * 4,
        out_specs=(any_spec,) * 4 + (smem_spec,),
        scratch_shapes=[
            pltpu.VMEM((3, 1, BLK), F32),
            pltpu.VMEM((1, ROWS), F32),
            pltpu.VMEM((KEYS_ROWS, ROWS), F32),
            pltpu.VMEM((3, KV, BLK, WIDTH), BF16),
            pltpu.VMEM((3, KV, BLK, WIDTH), BF16),
            pltpu.VMEM((KV, KEYS_WIDE, HD), BF16),
            pltpu.VMEM((KV, KEYS_WIDE, HD), BF16),
            pltpu.VMEM((KV, HD, KEYS_WIDE), BF16),
            pltpu.VMEM((KV, HD, KEYS_WIDE), BF16),
            pltpu.VMEM((2, KV, BLK, WIDTH), BF16),
            pltpu.VMEM((2, KV, BLK, WIDTH), BF16),
            pltpu.VMEM((KV, BLK, WIDTH), F32),
            pltpu.VMEM((SLOTS, PARTS, HD, ROWS), F32),
            pltpu.VMEM((SLOTS, PARTS, KEYS_ROWS, ROWS), F32),
            pltpu.VMEM((KEYS_ROWS, HD), F32),
            pltpu.VMEM((KEYS_ROWS, HD), F32),
            pltpu.VMEM((SLOTS, 4, GROUP, BLK), F32),
            pltpu.VMEM((3, KV, 4, GROUP, BLK), F32),
            pltpu.VMEM((2, KV, 4, GROUP, BLK), F32),
            pltpu.VMEM((KV, 2, GROUP, BLK), F32),
            pltpu.VMEM((2, KV, 2, GROUP, BLK), F32),
            pltpu.VMEM((2, GROUP, BLK), F32),
            pltpu.VMEM((SLOTS, PARTS, HD, ROWS), BF16),
            pltpu.VMEM((GROUP, BLK), F32),
            pltpu.VMEM((total_rounds, GROUP, BLK), F32),
            pltpu.VMEM((total_rounds, GROUP, BLK), F32),
            sems(2, KV),
            sems(2, KV),
            sems(2, 2, KV),
            sems(2, 2, KV),
            sems(2, 2, KV),
            sems(2, 2, KV),
            sems(2, 2, KV, PARTS),
            sems(2, 2, KV, PARTS),
            sems(2, KV),
            sems(2, KV),
            sems(2, total_rounds),
        ],
        compiler_params=pltpu.CompilerParams(
            collective_id=0, has_side_effects=True, vmem_limit_bytes=VMEM_LIMIT
        ),
        cost_estimate=pl.CostEstimate(
            flops=2 * 6 * UNITS * 1024 * KEYS * HD,
            bytes_accessed=11_000_000,
            transcendentals=UNITS * 1024 * KEYS,
        ),
    )(
        tanh.reshape(1, 1),
        tile_list[0].T,
        slot_range[0].T,
        keys,
        values,
        queries[0],
        cotangent[0],
        keys,
        values,
    )

    steps = 4
    rows = BLK // steps
    key_rows = -(-KEYS // (16 * steps)) * 16
    token_spec = pl.BlockSpec((rows, KV * WIDTH), lambda i: (i, 0))
    key_spec = pl.BlockSpec((key_rows, KV * HD), lambda i: (i, 0))
    specs = (token_spec, token_spec, key_spec, key_spec)
    attended, query_grad, key_grad, value_grad = pl.pallas_call(
        hand_on,
        out_shape=(
            jax.ShapeDtypeStruct((BLK, KV * WIDTH), BF16),
            jax.ShapeDtypeStruct((BLK, KV * WIDTH), BF16),
            jax.ShapeDtypeStruct((KEYS, KV * HD), BF16),
            jax.ShapeDtypeStruct((KEYS, KV * HD), BF16),
        ),
        grid=(steps,),
        in_specs=specs,
        out_specs=specs,
        compiler_params=pltpu.CompilerParams(vmem_limit_bytes=VMEM_LIMIT),
    )(attended, query_grad, key_out, value_out)
    return (
        attended[None],
        query_grad[None],
        key_grad[None, None],
        value_grad[None, None],
        gate_out.reshape(()),
    )


def solution(mesh):
    ring = mesh.shape["seq"]
    rounds = (ring.bit_length() - 1, mesh.shape["dp"].bit_length() - 1)
    in_specs = (
        P("dp", "seq", None),
        P("dp", "seq", None, None),
        P("dp", "seq", None, None),
        P("dp", "seq", None),
        P(),
        P("dp", None, None),
        P("dp", None, None),
    )
    out_specs = (
        P("dp", "seq", None),
        P("dp", "seq", None),
        P("dp", "seq", None, None),
        P("dp", "seq", None, None),
        P(),
    )
    return jax.shard_map(
        functools.partial(shards, ring, rounds),
        mesh=mesh,
        in_specs=in_specs,
        out_specs=out_specs,
        check_vma=False,
    )
```

```python
import functools

import jax
import jax.numpy as jnp
from jax import lax
from jax.experimental import pallas as pl
from jax.experimental.pallas import tpu as pltpu
from jax.sharding import PartitionSpec as P

KV = 4
GROUP = 8
HD = 128
BLK = 128
KEYS = 1601
KEYS_MAIN = 1600
KEYS_ROWS = 1616
KEYS_WIDE = 1664
WIDTH = GROUP * HD
HEADS = 4
PARTS = GROUP // HEADS
ROWS = HEADS * BLK
CUTS = ((0, 768), (768, 848))
UNITS = 3 * KV
LAG = 4
SLOTS = LAG + 1
FWD_SIDE = (2, 0, 1) * KV
BWD_SIDE = (2, 0, 1) * (KV - 1) + (0, 1, 2)
LOW = -1e30
VMEM_LIMIT = 64 * 1024 * 1024 - 65536
SCALE = HD**-0.5
LOG2E = 1.4426950408889634
FACTOR = SCALE * LOG2E
F32 = jnp.float32
BF16 = jnp.bfloat16
MESH = pl.DeviceIdType.MESH


def mm(a, b):
    return jnp.dot(a, b, preferred_element_type=F32)


def pieces(wide):
    return [wide[:, g * BLK : (g + 1) * BLK] for g in range(HEADS)]


def stack_rows(chunk):
    return jnp.concatenate(pieces(chunk), axis=0)


def turn(chunk):
    return jnp.concatenate([piece.T for piece in pieces(chunk)], axis=1)


def slot_tables():
    free, held, fwd, bwd = list(range(SLOTS)), {}, [], []
    for step in range(UNITS + LAG):
        if step < UNITS:
            held[step // 3, FWD_SIDE[step]] = free.pop(0)
            fwd.append(held[step // 3, FWD_SIDE[step]])
        if step >= LAG:
            old = step - LAG
            bwd.append(held.pop((old // 3, BWD_SIDE[old])))
            free.append(bwd[-1])
    return fwd, bwd


FWD_SLOT, BWD_SLOT = slot_tables()


def pick(table, index):
    found = jnp.int32(table[0])
    for place, value in enumerate(table[1:], 1):
        found = jnp.where(index == place, value, found)
    return found


def kernel(
    ring,
    rounds,
    gate_ref,
    list_ref,
    range_ref,
    ktail_ref,
    vtail_ref,
    q_hbm,
    cot_hbm,
    k_hbm,
    v_hbm,
    att_hbm,
    dq_hbm,
    dk_hbm,
    dv_hbm,
    gsum_ref,
    mask_ref,
    rmax,
    sbuf,
    qb,
    cb,
    kp,
    vp,
    kt,
    vt,
    ret_o,
    ret_q,
    own_o,
    onum,
    pbuf,
    dk_acc,
    dv_acc,
    stats,
    stats_out,
    stats_in,
    lse_out,
    lse_in,
    cvec,
    dot,
    gacc,
    gsend,
    grecv,
    s_kv,
    s_own,
    s_q,
    s_c,
    s_stat,
    s_lse,
    s_ro,
    s_rq,
    s_out,
    s_kvout,
    s_g,
):
    me = lax.axis_index("seq")
    dpi = lax.axis_index("dp")
    right = lax.rem(me + 1, ring)
    left = lax.rem(me + ring - 1, ring)
    tanh = gate_ref[0, 0]

    def cols(h):
        return pl.ds(pl.multiple_of(h * WIDTH, WIDTH), WIDTH)

    def to_side(d):
        return right if d == 0 else left

    def send_q(d, h):
        return pltpu.make_async_remote_copy(
            src_ref=q_hbm.at[:, cols(h)],
            dst_ref=qb.at[d, h],
            send_sem=s_q.at[0, d, h],
            recv_sem=s_q.at[1, d, h],
            device_id={"seq": to_side(d)},
            device_id_type=MESH,
        )

    def send_c(d, h):
        return pltpu.make_async_remote_copy(
            src_ref=cot_hbm.at[:, cols(h)],
            dst_ref=cb.at[d, h],
            send_sem=s_c.at[0, d, h],
            recv_sem=s_c.at[1, d, h],
            device_id={"seq": to_side(d)},
            device_id_type=MESH,
        )

    def send_stat(p, h):
        return pltpu.make_async_remote_copy(
            src_ref=stats_out.at[p, h],
            dst_ref=stats_in.at[1 - p, h],
            send_sem=s_stat.at[0, p, h],
            recv_sem=s_stat.at[1, 1 - p, h],
            device_id={"seq": to_side(1 - p)},
            device_id_type=MESH,
        )

    def send_lse(d, h):
        return pltpu.make_async_remote_copy(
            src_ref=lse_out.at[h],
            dst_ref=lse_in.at[d, h],
            send_sem=s_lse.at[0, d, h],
            recv_sem=s_lse.at[1, d, h],
            device_id={"seq": to_side(d)},
            device_id_type=MESH,
        )

    def chunk_lanes(c):
        return pl.ds(pl.multiple_of(c * ROWS, ROWS), ROWS)

    def send_ro(p, h, c):
        return pltpu.make_async_remote_copy(
            src_ref=cb.at[p, h, :, chunk_lanes(c)],
            dst_ref=ret_o.at[1 - p, h, :, chunk_lanes(c)],
            send_sem=s_ro.at[0, p, h, c],
            recv_sem=s_ro.at[1, 1 - p, h, c],
            device_id={"seq": to_side(1 - p)},
            device_id_type=MESH,
        )

    def send_rq(p, h, c):
        return pltpu.make_async_remote_copy(
            src_ref=qb.at[p, h, :, chunk_lanes(c)],
            dst_ref=ret_q.at[1 - p, h, :, chunk_lanes(c)],
            send_sem=s_rq.at[0, p, h, c],
            recv_sem=s_rq.at[1, 1 - p, h, c],
            device_id={"seq": to_side(1 - p)},
            device_id_type=MESH,
        )

    def gate_partner(r):
        name, place, bit = ("seq", me, r) if r < rounds[0] else ("dp", dpi, r - rounds[0])
        stride = 1 << bit
        return {name: place + stride * (1 - 2 * ((place // stride) % 2))}

    def send_gate(r):
        return pltpu.make_async_remote_copy(
            src_ref=gsend.at[r],
            dst_ref=grecv.at[r],
            send_sem=s_g.at[0, r],
            recv_sem=s_g.at[1, r],
            device_id=gate_partner(r),
            device_id_type=MESH,
        )

    own_q = lambda h: pltpu.make_async_copy(q_hbm.at[:, cols(h)], qb.at[2, h], s_own.at[0, h])
    own_c = lambda h: pltpu.make_async_copy(cot_hbm.at[:, cols(h)], cb.at[2, h], s_own.at[1, h])

    def load_kv(which, h):
        src, dst = ((k_hbm, kp), (v_hbm, vp))[which]
        lanes = pl.ds(pl.multiple_of(h * HD, HD), HD)
        return pltpu.make_async_copy(
            src.at[pl.ds(0, KEYS_MAIN), lanes],
            dst.at[h, pl.ds(0, KEYS_MAIN)],
            s_kv.at[which, h],
        )

    def store_kv(which, h):
        src, dst = ((kp, dk_hbm), (vp, dv_hbm))[which]
        return pltpu.make_async_copy(
            src.at[h, pl.ds(0, KEYS_ROWS)],
            dst.at[:, pl.ds(pl.multiple_of(h * HD, HD), HD)],
            s_kvout.at[which, h],
        )

    def store_att(h):
        return pltpu.make_async_copy(cb.at[2, h], att_hbm.at[:, cols(h)], s_out.at[0, h])

    def store_dq(h):
        return pltpu.make_async_copy(qb.at[2, h], dq_hbm.at[:, cols(h)], s_out.at[1, h])

    for h in range(KV):
        for which in range(2):
            load_kv(which, h).start()
    for h in range(KV):
        own_q(h).start()
        own_c(h).start()

    total_rounds = rounds[0] + rounds[1]
    barrier = pltpu.get_barrier_semaphore()
    for side in (left, right):
        pl.semaphore_signal(barrier, inc=1, device_id={"seq": side}, device_id_type=MESH)
    for r in range(total_rounds):
        pl.semaphore_signal(barrier, inc=1, device_id=gate_partner(r), device_id_type=MESH)
    pl.semaphore_wait(barrier, 2 + total_rounds)

    def send_inputs(h):
        for d in range(2):
            send_q(d, h).start()
        for d in range(2):
            send_c(d, h).start()

    send_inputs(0)
    gacc[...] = jnp.zeros_like(gacc)
    for p, (block, slot) in enumerate(((left, 1), (right, 1), (me, 0))):
        tokens = pl.ds(pl.multiple_of(block * BLK, BLK), BLK)
        first, last = range_ref[0:1, tokens], range_ref[1:2, tokens]
        listed = jnp.where(list_ref[slot, block] == me, 1.0, 0.0).astype(F32)
        mask_ref[p] = jnp.where((first <= slot) & (slot < last), 1.0, 0.0).astype(F32) * listed

    def prepare(h, _):
        for which in range(2):
            load_kv(which, h).wait()
        lanes = pl.ds(pl.multiple_of(h * HD, HD), HD)
        for tail, dst, flipped in ((ktail_ref, kp, kt), (vtail_ref, vp, vt)):
            rows = lax.broadcasted_iota(jnp.int32, (KEYS_ROWS - KEYS_MAIN, HD), 0)
            dst[h, KEYS_MAIN:KEYS_ROWS, :] = jnp.where(
                rows < KEYS - KEYS_MAIN, tail[:, lanes].astype(F32), 0.0
            ).astype(BF16)
            dst[h, KEYS_ROWS:, :] = jnp.zeros((KEYS_WIDE - KEYS_ROWS, HD), BF16)
            for j in range(KEYS_WIDE // HD):
                piece = dst[h, j * HD : (j + 1) * HD, :]
                flipped[h, :, j * HD : (j + 1) * HD] = piece.T
        return 0

    lax.fori_loop(0, KV, prepare, 0)

    def combine(h):
        send_stat(0, h).wait_recv()
        send_stat(1, h).wait_recv()
        mine = stats_out[2, h]
        low = stats_in[0, h]
        high = stats_in[1, h]
        top = jnp.maximum(jnp.maximum(mine[0], low[0]), high[0])
        shares = [one[1] * jnp.exp2(one[0] - top) for one in (mine, low, high)]
        whole = shares[0] + shares[1] + shares[2]
        some = whole > 0.0
        safe = jnp.where(some, whole, 1.0)
        delta = (shares[0] * mine[2] + shares[1] * low[2] + shares[2] * high[2]) / safe
        gamma = (shares[0] * mine[3] + shares[1] * low[3] + shares[2] * high[3]) / safe
        lse_out[h, 0] = jnp.where(some, top + jnp.log(safe) * LOG2E, 0.0)
        lse_out[h, 1] = jnp.where(some, delta, 0.0)
        gacc[...] += jnp.where(some, gamma, 0.0)
        for d in range(2):
            send_lse(d, h).start()

    def finalize(h):
        for p in range(2):
            for c in range(PARTS):
                send_ro(p, h, c).wait_recv()
                send_rq(p, h, c).wait_recv()
        cb[2, h] = (own_o[h] + ret_o[0, h].astype(F32) + ret_o[1, h].astype(F32)).astype(BF16)
        qb[2, h] = (
            qb[2, h].astype(F32) + ret_q[0, h].astype(F32) + ret_q[1, h].astype(F32)
        ).astype(BF16)
        store_att(h).start()
        store_dq(h).start()

    def side_of(u):
        return lax.rem(u + 2, 3)

    def back_side(u):
        return lax.rem(jnp.where(u < UNITS - 3, u + 2, u), 3)

    def chunk(u, c, scoring, weighing, backing):
        if scoring:
            ahead = jnp.int32(0) if not weighing else jnp.minimum(u * PARTS + c + 1, UNITS * PARTS - 1)
            ua, ca = ahead // PARTS, lax.rem(ahead, PARTS)
            ha, pa = ua // 3, side_of(ua)
            query_ahead = turn(qb[pa, ha, :, chunk_lanes(ca)])
            next_max = None
        if weighing:
            h, p, slot = u // 3, side_of(u), pick(FWD_SLOT, u)
            row_max = rmax[...] * FACTOR
            total = jnp.zeros((1, ROWS), F32)
            out = jnp.zeros((HD, ROWS), F32)
        if backing:
            ub = u - LAG
            hb, pb, slotb = ub // 3, back_side(ub), pick(BWD_SLOT, ub)
            lanes = chunk_lanes(c)
            query = stack_rows(qb[pb, hb, :, lanes])
            grad = (tanh * stack_rows(cb[pb, hb, :, lanes]).astype(F32)).astype(BF16)
            grad_t = dot[slotb, c]
            rows = [cvec[i, pl.ds(HEADS * c + g, 1), :] for i in range(2) for g in range(HEADS)]
            weight = jnp.concatenate(rows[:HEADS], axis=1)
            delta = jnp.concatenate(rows[HEADS:], axis=1)
            turned = jnp.zeros((HD, ROWS), F32)
        for start, size in CUTS:
            keys = slice(start, start + size)
            if backing:
                probs = pbuf[slotb, c, keys, :] * weight
                prob_grad = mm(vp[hb, keys, :], grad_t)
                score_grad = (probs * (prob_grad - delta)).astype(BF16)
                dv_acc[keys, :] += mm(probs.astype(BF16), grad)
                dk_acc[keys, :] += mm(score_grad, query)
                turned = turned + mm(kt[hb, :, keys], score_grad)
            if weighing:
                fresh = jnp.exp2(sbuf[keys, :] * FACTOR - row_max)
                pbuf[slot, c, keys, :] = fresh
                total = total + jnp.sum(fresh, axis=0, keepdims=True)
                out = out + mm(vt[h, :, keys], fresh.astype(BF16))
            if scoring:
                scores = mm(kp[ha, keys, :], query_ahead)
                if start + size > KEYS:
                    position = lax.broadcasted_iota(jnp.int32, scores.shape, 0)
                    scores = jnp.where(position < KEYS - start, scores, LOW)
                sbuf[keys, :] = scores
                part = jnp.max(scores, axis=0, keepdims=True)
                next_max = part if next_max is None else jnp.maximum(next_max, part)
        if weighing:
            onum[slot, c] = out
            cot = turn(cb[p, h, :, chunk_lanes(c)].astype(F32))
            fresh_grad = (tanh * cot).astype(BF16)
            dot[slot, c] = fresh_grad
            deltas = jnp.sum(fresh_grad.astype(F32) * out, axis=0, keepdims=True) / total
            gammas = jnp.sum(cot * out, axis=0, keepdims=True) / total
            for kind, row in enumerate((row_max, total, deltas, gammas)):
                for g, piece in enumerate(pieces(row)):
                    stats[slot, kind, pl.ds(HEADS * c + g, 1), :] = piece
        if scoring:
            rmax[...] = next_max
        if backing:
            turned = turned * SCALE
            part = onum[slotb, c] * (weight * tanh)
            part = turn(part)
            qb[pb, hb, :, lanes] = turn(turned).astype(BF16)

            for d in range(2):

                @pl.when(pb == d)
                def _():
                    cb[d, hb, :, lanes] = part.astype(BF16)
                    send_ro(d, hb, c).start()
                    send_rq(d, hb, c).start()

            @pl.when(pb == 2)
            def _():
                own_o[hb, :, lanes] = part

    def wait_query(u):
        h, p = u // 3, side_of(u)
        for d in range(2):

            @pl.when(p == d)
            def _():
                send_q(d, h).wait_recv()

        @pl.when(p == 2)
        def _():
            own_q(h).wait()

    def wait_cotangent(u):
        h, p = u // 3, side_of(u)
        for d in range(2):

            @pl.when(p == d)
            def _():
                send_c(d, h).wait_recv()

        @pl.when(p == 2)
        def _():
            own_c(h).wait()

        for later, place in ((1, 1), (2, 4), (3, 6)):

            @pl.when(u == place)
            def _():
                send_inputs(later)

    def forward_end(u):
        h, p, slot = u // 3, side_of(u), pick(FWD_SLOT, u)
        on = mask_ref[p] > 0.0
        for kind, fill in enumerate((LOW, 0.0, 0.0, 0.0)):
            stats_out[p, h, kind] = jnp.where(on, stats[slot, kind], fill)
        for d in range(2):

            @pl.when(p == d)
            def _():
                send_stat(d, h).start()

    def backward_start(u):
        h, p, slot = u // 3, back_side(u), pick(BWD_SLOT, u)
        on = mask_ref[p] > 0.0
        for d in range(2):

            @pl.when(p == d)
            def _():
                send_lse(d, h).wait_recv()
                cvec[0] = jnp.where(on, jnp.exp2(stats[slot, 0] - lse_in[d, h, 0]), 0.0)
                cvec[1] = lse_in[d, h, 1]

        @pl.when(p == 2)
        def _():
            cvec[0] = jnp.where(on, jnp.exp2(stats[slot, 0] - lse_out[h, 0]), 0.0)
            cvec[1] = lse_out[h, 1]

        @pl.when(lax.rem(u, 3) == 0)
        def _():
            dk_acc[...] = jnp.zeros_like(dk_acc)
            dv_acc[...] = jnp.zeros_like(dv_acc)

    def backward_end(u):
        h = u // 3

        @pl.when(lax.rem(u, 3) == 2)
        def _():
            kp[h, :KEYS_ROWS, :] = (dk_acc[...] * SCALE).astype(BF16)
            vp[h, :KEYS_ROWS, :] = dv_acc[...].astype(BF16)
            for which in range(2):
                store_kv(which, h).start()

    def chunk_events(u, c):
        @pl.when((u >= 3) & (u <= UNITS) & (u % 3 == 0) & (c == PARTS // 2))
        def _():
            combine(u // 3 - 1)

    def step_events(u):
        @pl.when((u >= 9) & (u % 3 == 0))
        def _():
            finalize(u // 3 - 3)

    def step(u, backing):
        step_events(u)
        wait_cotangent(u)
        if backing:
            backward_start(u - LAG)

        def one(c, x):
            chunk_events(u, c)

            @pl.when((c == PARTS - 1) & (u < UNITS - 1))
            def _():
                wait_query(u + 1)

            chunk(u, c, True, True, backing)
            return x

        lax.fori_loop(0, PARTS, one, 0)
        forward_end(u)
        if backing:
            backward_end(u - LAG)
        return 0

    def gate_round(r):
        if r > 0:
            send_gate(r - 1).wait_recv()
            gacc[...] += grecv[r - 1]
        if r < total_rounds:
            gsend[r] = gacc[...]
            send_gate(r).start()

    def tail_step(u, _):
        step_events(u)
        backward_start(u - LAG)

        def one(c, x):
            chunk_events(u, c)
            chunk(u, c, False, False, True)
            place = (u - UNITS) * PARTS + c
            for r in range(total_rounds):

                @pl.when(place == 1 + r)
                def _():
                    gate_round(r)

            return x

        lax.fori_loop(0, PARTS, one, 0)
        backward_end(u - LAG)
        return 0

    wait_query(jnp.int32(0))
    chunk(0, 0, True, False, False)
    lax.fori_loop(0, LAG, lambda u, x: step(u, False), 0)
    lax.fori_loop(LAG, UNITS, lambda u, x: step(u, True), 0)
    lax.fori_loop(UNITS, UNITS + LAG, tail_step, 0)
    gate_round(total_rounds)
    finalize(KV - 1)
    gsum_ref[0, 0] = (1.0 - tanh * tanh) * jnp.sum(gacc[...])

    for r in range(total_rounds):
        send_gate(r).wait_send()
    for h in range(KV):
        for d in range(2):
            send_q(d, h).wait_send()
            send_c(d, h).wait_send()
            send_stat(d, h).wait_send()
            send_lse(d, h).wait_send()
            for c in range(PARTS):
                send_ro(d, h, c).wait_send()
                send_rq(d, h, c).wait_send()
            store_kv(d, h).wait()
        store_att(h).wait()
        store_dq(h).wait()


def hand_on(*refs):
    count = len(refs) // 2
    for source, target in zip(refs[:count], refs[count:]):
        target[...] = source[...]


def shards(ring, rounds, queries, image_keys, image_values, cotangent, gate, tile_list, slot_range):
    keys, values = image_keys[0, 0], image_values[0, 0]
    tanh = jnp.tanh(gate)
    any_spec = pl.BlockSpec(memory_space=pl.ANY)
    smem_spec = pl.BlockSpec(memory_space=pltpu.SMEM)
    tail_rows = KEYS_ROWS - KEYS_MAIN
    tail_spec = pl.BlockSpec((tail_rows, KV * HD), lambda i: (KEYS_MAIN // tail_rows, 0))
    vmem_spec = pl.BlockSpec(memory_space=pltpu.VMEM)
    sems = lambda *shape: pltpu.SemaphoreType.DMA(shape)
    total_rounds = rounds[0] + rounds[1]
    attended, query_grad, key_out, value_out, gate_out = pl.pallas_call(
        functools.partial(kernel, ring, rounds),
        out_shape=(
            jax.ShapeDtypeStruct((BLK, KV * WIDTH), BF16),
            jax.ShapeDtypeStruct((BLK, KV * WIDTH), BF16),
            jax.ShapeDtypeStruct((KEYS_ROWS, KV * HD), BF16),
            jax.ShapeDtypeStruct((KEYS_ROWS, KV * HD), BF16),
            jax.ShapeDtypeStruct((1, 1), F32),
        ),
        grid=(1,),
        in_specs=[smem_spec, smem_spec, vmem_spec, tail_spec, tail_spec] + [any_spec] * 4,
        out_specs=(any_spec,) * 4 + (smem_spec,),
        scratch_shapes=[
            pltpu.VMEM((3, 1, BLK), F32),
            pltpu.VMEM((1, ROWS), F32),
            pltpu.VMEM((KEYS_ROWS, ROWS), F32),
            pltpu.VMEM((3, KV, BLK, WIDTH), BF16),
            pltpu.VMEM((3, KV, BLK, WIDTH), BF16),
            pltpu.VMEM((KV, KEYS_WIDE, HD), BF16),
            pltpu.VMEM((KV, KEYS_WIDE, HD), BF16),
            pltpu.VMEM((KV, HD, KEYS_WIDE), BF16),
            pltpu.VMEM((KV, HD, KEYS_WIDE), BF16),
            pltpu.VMEM((2, KV, BLK, WIDTH), BF16),
            pltpu.VMEM((2, KV, BLK, WIDTH), BF16),
            pltpu.VMEM((KV, BLK, WIDTH), F32),
            pltpu.VMEM((SLOTS, PARTS, HD, ROWS), F32),
            pltpu.VMEM((SLOTS, PARTS, KEYS_ROWS, ROWS), F32),
            pltpu.VMEM((KEYS_ROWS, HD), F32),
            pltpu.VMEM((KEYS_ROWS, HD), F32),
            pltpu.VMEM((SLOTS, 4, GROUP, BLK), F32),
            pltpu.VMEM((3, KV, 4, GROUP, BLK), F32),
            pltpu.VMEM((2, KV, 4, GROUP, BLK), F32),
            pltpu.VMEM((KV, 2, GROUP, BLK), F32),
            pltpu.VMEM((2, KV, 2, GROUP, BLK), F32),
            pltpu.VMEM((2, GROUP, BLK), F32),
            pltpu.VMEM((SLOTS, PARTS, HD, ROWS), BF16),
            pltpu.VMEM((GROUP, BLK), F32),
            pltpu.VMEM((total_rounds, GROUP, BLK), F32),
            pltpu.VMEM((total_rounds, GROUP, BLK), F32),
            sems(2, KV),
            sems(2, KV),
            sems(2, 2, KV),
            sems(2, 2, KV),
            sems(2, 2, KV),
            sems(2, 2, KV),
            sems(2, 2, KV, PARTS),
            sems(2, 2, KV, PARTS),
            sems(2, KV),
            sems(2, KV),
            sems(2, total_rounds),
        ],
        compiler_params=pltpu.CompilerParams(
            collective_id=0, has_side_effects=True, vmem_limit_bytes=VMEM_LIMIT
        ),
        cost_estimate=pl.CostEstimate(
            flops=2 * 6 * UNITS * 1024 * KEYS * HD,
            bytes_accessed=11_000_000,
            transcendentals=UNITS * 1024 * KEYS,
        ),
    )(
        tanh.reshape(1, 1),
        tile_list[0].T,
        slot_range[0].T,
        keys,
        values,
        queries[0],
        cotangent[0],
        keys,
        values,
    )

    steps = 4
    rows = BLK // steps
    key_rows = -(-KEYS // (16 * steps)) * 16
    token_spec = pl.BlockSpec((rows, KV * WIDTH), lambda i: (i, 0))
    key_spec = pl.BlockSpec((key_rows, KV * HD), lambda i: (i, 0))
    specs = (token_spec, token_spec, key_spec, key_spec)
    attended, query_grad, key_grad, value_grad = pl.pallas_call(
        hand_on,
        out_shape=(
            jax.ShapeDtypeStruct((BLK, KV * WIDTH), BF16),
            jax.ShapeDtypeStruct((BLK, KV * WIDTH), BF16),
            jax.ShapeDtypeStruct((KEYS, KV * HD), BF16),
            jax.ShapeDtypeStruct((KEYS, KV * HD), BF16),
        ),
        grid=(steps,),
        in_specs=specs,
        out_specs=specs,
        compiler_params=pltpu.CompilerParams(vmem_limit_bytes=VMEM_LIMIT),
    )(attended, query_grad, key_out, value_out)
    return (
        attended[None],
        query_grad[None],
        key_grad[None, None],
        value_grad[None, None],
        gate_out.reshape(()),
    )


def solution(mesh):
    ring = mesh.shape["seq"]
    rounds = (ring.bit_length() - 1, mesh.shape["dp"].bit_length() - 1)
    in_specs = (
        P("dp", "seq", None),
        P("dp", "seq", None, None),
        P("dp", "seq", None, None),
        P("dp", "seq", None),
        P(),
        P("dp", None, None),
        P("dp", None, None),
    )
    out_specs = (
        P("dp", "seq", None),
        P("dp", "seq", None),
        P("dp", "seq", None, None),
        P("dp", "seq", None, None),
        P(),
    )
    return jax.shard_map(
        functools.partial(shards, ring, rounds),
        mesh=mesh,
        in_specs=in_specs,
        out_specs=out_specs,
        check_vma=False,
    )
```

```python
import functools

import jax
import jax.numpy as jnp
from jax import lax
from jax.experimental import pallas as pl
from jax.experimental.pallas import tpu as pltpu
from jax.sharding import PartitionSpec as P

KV = 4
GROUP = 8
HD = 128
BLK = 128
KEYS = 1601
KEYS_MAIN = 1600
KEYS_ROWS = 1616
KEYS_WIDE = 1664
WIDTH = GROUP * HD
HEADS = 4
PARTS = GROUP // HEADS
ROWS = HEADS * BLK
CUTS = ((0, 1616),)
UNITS = 3 * KV
LAG = 4
SLOTS = LAG + 1
FWD_SIDE = (2, 0, 1) * KV
BWD_SIDE = (2, 0, 1) * (KV - 1) + (0, 1, 2)
LOW = -1e30
VMEM_LIMIT = 64 * 1024 * 1024 - 65536
SCALE = HD**-0.5
LOG2E = 1.4426950408889634
FACTOR = SCALE * LOG2E
F32 = jnp.float32
BF16 = jnp.bfloat16
MESH = pl.DeviceIdType.MESH


def mm(a, b):
    return jnp.dot(a, b, preferred_element_type=F32)


def pieces(wide):
    return [wide[:, g * BLK : (g + 1) * BLK] for g in range(HEADS)]


def stack_rows(chunk):
    return jnp.concatenate(pieces(chunk), axis=0)


def turn(chunk):
    return jnp.concatenate([piece.T for piece in pieces(chunk)], axis=1)


def slot_tables():
    free, held, fwd, bwd = list(range(SLOTS)), {}, [], []
    for step in range(UNITS + LAG):
        if step < UNITS:
            held[step // 3, FWD_SIDE[step]] = free.pop(0)
            fwd.append(held[step // 3, FWD_SIDE[step]])
        if step >= LAG:
            old = step - LAG
            bwd.append(held.pop((old // 3, BWD_SIDE[old])))
            free.append(bwd[-1])
    return fwd, bwd


FWD_SLOT, BWD_SLOT = slot_tables()


def pick(table, index):
    found = jnp.int32(table[0])
    for place, value in enumerate(table[1:], 1):
        found = jnp.where(index == place, value, found)
    return found


def kernel(
    ring,
    rounds,
    gate_ref,
    list_ref,
    range_ref,
    ktail_ref,
    vtail_ref,
    q_hbm,
    cot_hbm,
    k_hbm,
    v_hbm,
    att_hbm,
    dq_hbm,
    dk_hbm,
    dv_hbm,
    gsum_ref,
    mask_ref,
    rmax,
    qb,
    cb,
    kp,
    vp,
    kt,
    vt,
    ret_o,
    ret_q,
    own_o,
    onum,
    pbuf,
    dk_acc,
    dv_acc,
    stats,
    stats_out,
    stats_in,
    lse_out,
    lse_in,
    cvec,
    dot,
    gacc,
    gsend,
    grecv,
    s_kv,
    s_own,
    s_q,
    s_c,
    s_stat,
    s_lse,
    s_ro,
    s_rq,
    s_out,
    s_kvout,
    s_g,
):
    me = lax.axis_index("seq")
    dpi = lax.axis_index("dp")
    right = lax.rem(me + 1, ring)
    left = lax.rem(me + ring - 1, ring)
    tanh = gate_ref[0, 0]

    def cols(h):
        return pl.ds(pl.multiple_of(h * WIDTH, WIDTH), WIDTH)

    def to_side(d):
        return right if d == 0 else left

    def send_q(d, h):
        return pltpu.make_async_remote_copy(
            src_ref=q_hbm.at[:, cols(h)],
            dst_ref=qb.at[d, h],
            send_sem=s_q.at[0, d, h],
            recv_sem=s_q.at[1, d, h],
            device_id={"seq": to_side(d)},
            device_id_type=MESH,
        )

    def send_c(d, h):
        return pltpu.make_async_remote_copy(
            src_ref=cot_hbm.at[:, cols(h)],
            dst_ref=cb.at[d, h],
            send_sem=s_c.at[0, d, h],
            recv_sem=s_c.at[1, d, h],
            device_id={"seq": to_side(d)},
            device_id_type=MESH,
        )

    def send_stat(p, h):
        return pltpu.make_async_remote_copy(
            src_ref=stats_out.at[p, h],
            dst_ref=stats_in.at[1 - p, h],
            send_sem=s_stat.at[0, p, h],
            recv_sem=s_stat.at[1, 1 - p, h],
            device_id={"seq": to_side(1 - p)},
            device_id_type=MESH,
        )

    def send_lse(d, h):
        return pltpu.make_async_remote_copy(
            src_ref=lse_out.at[h],
            dst_ref=lse_in.at[d, h],
            send_sem=s_lse.at[0, d, h],
            recv_sem=s_lse.at[1, d, h],
            device_id={"seq": to_side(d)},
            device_id_type=MESH,
        )

    def chunk_lanes(c):
        return pl.ds(pl.multiple_of(c * ROWS, ROWS), ROWS)

    def send_ro(p, h, c):
        return pltpu.make_async_remote_copy(
            src_ref=cb.at[p, h, :, chunk_lanes(c)],
            dst_ref=ret_o.at[1 - p, h, :, chunk_lanes(c)],
            send_sem=s_ro.at[0, p, h, c],
            recv_sem=s_ro.at[1, 1 - p, h, c],
            device_id={"seq": to_side(1 - p)},
            device_id_type=MESH,
        )

    def send_rq(p, h, c):
        return pltpu.make_async_remote_copy(
            src_ref=qb.at[p, h, :, chunk_lanes(c)],
            dst_ref=ret_q.at[1 - p, h, :, chunk_lanes(c)],
            send_sem=s_rq.at[0, p, h, c],
            recv_sem=s_rq.at[1, 1 - p, h, c],
            device_id={"seq": to_side(1 - p)},
            device_id_type=MESH,
        )

    def gate_partner(r):
        name, place, bit = ("seq", me, r) if r < rounds[0] else ("dp", dpi, r - rounds[0])
        stride = 1 << bit
        return {name: place + stride * (1 - 2 * ((place // stride) % 2))}

    def send_gate(r):
        return pltpu.make_async_remote_copy(
            src_ref=gsend.at[r],
            dst_ref=grecv.at[r],
            send_sem=s_g.at[0, r],
            recv_sem=s_g.at[1, r],
            device_id=gate_partner(r),
            device_id_type=MESH,
        )

    own_q = lambda h: pltpu.make_async_copy(q_hbm.at[:, cols(h)], qb.at[2, h], s_own.at[0, h])
    own_c = lambda h: pltpu.make_async_copy(cot_hbm.at[:, cols(h)], cb.at[2, h], s_own.at[1, h])

    def load_kv(which, h):
        src, dst = ((k_hbm, kp), (v_hbm, vp))[which]
        lanes = pl.ds(pl.multiple_of(h * HD, HD), HD)
        return pltpu.make_async_copy(
            src.at[pl.ds(0, KEYS_MAIN), lanes],
            dst.at[h, pl.ds(0, KEYS_MAIN)],
            s_kv.at[which, h],
        )

    def store_kv(which, h):
        src, dst = ((kp, dk_hbm), (vp, dv_hbm))[which]
        return pltpu.make_async_copy(
            src.at[h, pl.ds(0, KEYS_ROWS)],
            dst.at[:, pl.ds(pl.multiple_of(h * HD, HD), HD)],
            s_kvout.at[which, h],
        )

    def store_att(h):
        return pltpu.make_async_copy(cb.at[2, h], att_hbm.at[:, cols(h)], s_out.at[0, h])

    def store_dq(h):
        return pltpu.make_async_copy(qb.at[2, h], dq_hbm.at[:, cols(h)], s_out.at[1, h])

    for h in range(KV):
        for which in range(2):
            load_kv(which, h).start()
    for h in range(KV):
        own_q(h).start()
        own_c(h).start()

    total_rounds = rounds[0] + rounds[1]
    barrier = pltpu.get_barrier_semaphore()
    for side in (left, right):
        pl.semaphore_signal(barrier, inc=1, device_id={"seq": side}, device_id_type=MESH)
    for r in range(total_rounds):
        pl.semaphore_signal(barrier, inc=1, device_id=gate_partner(r), device_id_type=MESH)
    pl.semaphore_wait(barrier, 2 + total_rounds)

    for send in (send_q, send_c):
        for d in range(2):
            send(d, 0).start()

    gacc[...] = jnp.zeros_like(gacc)
    for p, (block, slot) in enumerate(((left, 1), (right, 1), (me, 0))):
        tokens = pl.ds(pl.multiple_of(block * BLK, BLK), BLK)
        first, last = range_ref[0:1, tokens], range_ref[1:2, tokens]
        listed = jnp.where(list_ref[slot, block] == me, 1.0, 0.0).astype(F32)
        mask_ref[p] = jnp.where((first <= slot) & (slot < last), 1.0, 0.0).astype(F32) * listed

    def prepare(h, _):
        for which in range(2):
            load_kv(which, h).wait()
        lanes = pl.ds(pl.multiple_of(h * HD, HD), HD)
        for tail, dst, flipped in ((ktail_ref, kp, kt), (vtail_ref, vp, vt)):
            rows = lax.broadcasted_iota(jnp.int32, (KEYS_ROWS - KEYS_MAIN, HD), 0)
            dst[h, KEYS_MAIN:KEYS_ROWS, :] = jnp.where(
                rows < KEYS - KEYS_MAIN, tail[:, lanes].astype(F32), 0.0
            ).astype(BF16)
            dst[h, KEYS_ROWS:, :] = jnp.zeros((KEYS_WIDE - KEYS_ROWS, HD), BF16)
            for j in range(KEYS_WIDE // HD):
                piece = dst[h, j * HD : (j + 1) * HD, :]
                flipped[h, :, j * HD : (j + 1) * HD] = piece.T
        return 0

    lax.fori_loop(0, KV, prepare, 0)

    def combine(h):
        send_stat(0, h).wait_recv()
        send_stat(1, h).wait_recv()
        mine = stats_out[2, h]
        low = stats_in[0, h]
        high = stats_in[1, h]
        top = jnp.maximum(jnp.maximum(mine[0], low[0]), high[0])
        shares = [one[1] * jnp.exp2(one[0] - top) for one in (mine, low, high)]
        whole = shares[0] + shares[1] + shares[2]
        some = whole > 0.0
        safe = jnp.where(some, whole, 1.0)
        delta = (shares[0] * mine[2] + shares[1] * low[2] + shares[2] * high[2]) / safe
        gamma = (shares[0] * mine[3] + shares[1] * low[3] + shares[2] * high[3]) / safe
        lse_out[h, 0] = jnp.where(some, top + jnp.log(safe) * LOG2E, 0.0)
        lse_out[h, 1] = jnp.where(some, delta, 0.0)
        gacc[...] += jnp.where(some, gamma, 0.0)
        for d in range(2):
            send_lse(d, h).start()

    def finalize(h):
        for p in range(2):
            for c in range(PARTS):
                send_ro(p, h, c).wait_recv()
                send_rq(p, h, c).wait_recv()
        cb[2, h] = (own_o[h] + ret_o[0, h].astype(F32) + ret_o[1, h].astype(F32)).astype(BF16)
        qb[2, h] = (
            qb[2, h].astype(F32) + ret_q[0, h].astype(F32) + ret_q[1, h].astype(F32)
        ).astype(BF16)
        store_att(h).start()
        store_dq(h).start()

    def side_of(u):
        return lax.rem(u + 2, 3)

    def back_side(u):
        return lax.rem(jnp.where(u < UNITS - 3, u + 2, u), 3)

    def chunk(u, c, scoring, weighing, backing):
        if scoring:
            ahead = jnp.int32(0) if not weighing else jnp.minimum(u * PARTS + c + 1, UNITS * PARTS - 1)
            ua, ca = ahead // PARTS, lax.rem(ahead, PARTS)
            ha, pa = ua // 3, side_of(ua)
            slota = pick(FWD_SLOT, ua)
            query_ahead = turn(qb[pa, ha, :, chunk_lanes(ca)])
            next_max = None
        if weighing:
            h, p, slot = u // 3, side_of(u), pick(FWD_SLOT, u)
            row_max = rmax[...]
            total = jnp.zeros((1, ROWS), F32)
            out = jnp.zeros((HD, ROWS), F32)
        if backing:
            ub = u - LAG
            hb, pb, slotb = ub // 3, back_side(ub), pick(BWD_SLOT, ub)
            lanes = chunk_lanes(c)
            query = stack_rows(qb[pb, hb, :, lanes])
            grad = (tanh * stack_rows(cb[pb, hb, :, lanes]).astype(F32)).astype(BF16)
            grad_t = dot[slotb, c]
            lse, delta, weight = (
                jnp.concatenate(
                    [cvec[i, pl.ds(HEADS * c + g, 1), :] for g in range(HEADS)], axis=1
                )
                for i in range(3)
            )
            turned = jnp.zeros((HD, ROWS), F32)
        for start, size in CUTS:
            keys = slice(start, start + size)
            if backing:
                probs = jnp.exp2(pbuf[slotb, c, keys, :] - lse)
                prob_grad = mm(vp[hb, keys, :], grad_t)
                score_grad = (probs * (prob_grad - delta)).astype(BF16)
                dv_acc[keys, :] += mm(probs.astype(BF16), grad)
                dk_acc[keys, :] += mm(score_grad, query)
                turned = turned + mm(kt[hb, :, keys], score_grad)
            if weighing:
                fresh = jnp.exp2(pbuf[slot, c, keys, :] - row_max)
                total = total + jnp.sum(fresh, axis=0, keepdims=True)
                out = out + mm(vt[h, :, keys], fresh.astype(BF16))
            if scoring:
                scores = mm(kp[ha, keys, :], query_ahead) * FACTOR
                if start + size > KEYS:
                    position = lax.broadcasted_iota(jnp.int32, scores.shape, 0)
                    scores = jnp.where(position < KEYS - start, scores, LOW)
                pbuf[slota, ca, keys, :] = scores
                part = jnp.max(scores, axis=0, keepdims=True)
                next_max = part if next_max is None else jnp.maximum(next_max, part)
        if weighing:
            onum[slot, c] = out
            cot = turn(cb[p, h, :, chunk_lanes(c)].astype(F32))
            fresh_grad = (tanh * cot).astype(BF16)
            dot[slot, c] = fresh_grad
            deltas = jnp.sum(fresh_grad.astype(F32) * out, axis=0, keepdims=True) / total
            gammas = jnp.sum(cot * out, axis=0, keepdims=True) / total
            for kind, row in enumerate((row_max, total, deltas, gammas)):
                for g, piece in enumerate(pieces(row)):
                    stats[slot, kind, pl.ds(HEADS * c + g, 1), :] = piece
        if scoring:
            rmax[...] = next_max
        if backing:
            turned = turned * SCALE
            part = onum[slotb, c] * (weight * tanh)
            part = turn(part)
            qb[pb, hb, :, lanes] = turn(turned).astype(BF16)

            for d in range(2):

                @pl.when(pb == d)
                def _():
                    cb[d, hb, :, lanes] = part.astype(BF16)
                    send_ro(d, hb, c).start()
                    send_rq(d, hb, c).start()

            @pl.when(pb == 2)
            def _():
                own_o[hb, :, lanes] = part

    def wait_query(u):
        h, p = u // 3, side_of(u)
        for d in range(2):

            @pl.when(p == d)
            def _():
                send_q(d, h).wait_recv()

        @pl.when(p == 2)
        def _():
            own_q(h).wait()

    def wait_cotangent(u):
        h, p = u // 3, side_of(u)
        for d in range(2):

            @pl.when(p == d)
            def _():
                send_c(d, h).wait_recv()

        @pl.when(p == 2)
        def _():
            own_c(h).wait()

        for later, place, sends in (
            (1, 1, (send_q, send_c)),
            (2, 4, (send_q, send_c)),
            (3, 5, (send_q,)),
            (3, 6, (send_c,)),
        ):

            @pl.when(u == place)
            def _():
                for send in sends:
                    for d in range(2):
                        send(d, later).start()

    def forward_end(u):
        h, p, slot = u // 3, side_of(u), pick(FWD_SLOT, u)
        on = mask_ref[p] > 0.0
        for kind, fill in enumerate((LOW, 0.0, 0.0, 0.0)):
            stats_out[p, h, kind] = jnp.where(on, stats[slot, kind], fill)
        for d in range(2):

            @pl.when(p == d)
            def _():
                send_stat(d, h).start()

    def backward_start(u):
        h, p, slot = u // 3, back_side(u), pick(BWD_SLOT, u)

        def meet(lse, delta):
            on = mask_ref[p] > 0.0
            cvec[0] = jnp.where(on, lse, -LOW)
            cvec[1] = delta
            cvec[2] = jnp.where(on, jnp.exp2(stats[slot, 0] - lse), 0.0)

        for d in range(2):

            @pl.when(p == d)
            def _():
                send_lse(d, h).wait_recv()
                meet(lse_in[d, h, 0], lse_in[d, h, 1])

        @pl.when(p == 2)
        def _():
            meet(lse_out[h, 0], lse_out[h, 1])

        @pl.when(lax.rem(u, 3) == 0)
        def _():
            dk_acc[...] = jnp.zeros_like(dk_acc)
            dv_acc[...] = jnp.zeros_like(dv_acc)

    def backward_end(u):
        h = u // 3

        @pl.when(lax.rem(u, 3) == 2)
        def _():
            kp[h, :KEYS_ROWS, :] = (dk_acc[...] * SCALE).astype(BF16)
            vp[h, :KEYS_ROWS, :] = dv_acc[...].astype(BF16)
            for which in range(2):
                store_kv(which, h).start()

    def chunk_events(u, c):
        @pl.when((u >= 3) & (u <= UNITS) & (u % 3 == 0) & (c == PARTS // 2))
        def _():
            combine(u // 3 - 1)

    def step_events(u):
        @pl.when((u >= 9) & (u % 3 == 0))
        def _():
            finalize(u // 3 - 3)

    def step(u, backing):
        step_events(u)
        wait_cotangent(u)
        if backing:
            backward_start(u - LAG)

        def one(c, x):
            chunk_events(u, c)

            @pl.when((c == PARTS - 1) & (u < UNITS - 1))
            def _():
                wait_query(u + 1)

            chunk(u, c, True, True, backing)
            return x

        lax.fori_loop(0, PARTS, one, 0)
        forward_end(u)
        if backing:
            backward_end(u - LAG)
        return 0

    def gate_round(r):
        if r > 0:
            send_gate(r - 1).wait_recv()
            gacc[...] += grecv[r - 1]
        if r < total_rounds:
            gsend[r] = gacc[...]
            send_gate(r).start()

    def tail_step(u, _):
        step_events(u)
        backward_start(u - LAG)

        def one(c, x):
            chunk_events(u, c)
            chunk(u, c, False, False, True)
            place = (u - UNITS) * PARTS + c
            for r in range(total_rounds):

                @pl.when(place == 1 + r)
                def _():
                    gate_round(r)

            return x

        lax.fori_loop(0, PARTS, one, 0)
        backward_end(u - LAG)
        return 0

    wait_query(jnp.int32(0))
    chunk(0, 0, True, False, False)
    lax.fori_loop(0, LAG, lambda u, x: step(u, False), 0)
    lax.fori_loop(LAG, UNITS, lambda u, x: step(u, True), 0)
    lax.fori_loop(UNITS, UNITS + LAG, tail_step, 0)
    gate_round(total_rounds)
    finalize(KV - 1)
    gsum_ref[0, 0] = (1.0 - tanh * tanh) * jnp.sum(gacc[...])

    for r in range(total_rounds):
        send_gate(r).wait_send()
    for h in range(KV):
        for d in range(2):
            send_q(d, h).wait_send()
            send_c(d, h).wait_send()
            send_stat(d, h).wait_send()
            send_lse(d, h).wait_send()
            for c in range(PARTS):
                send_ro(d, h, c).wait_send()
                send_rq(d, h, c).wait_send()
            store_kv(d, h).wait()
        store_att(h).wait()
        store_dq(h).wait()


def hand_on(*refs):
    count = len(refs) // 2
    for source, target in zip(refs[:count], refs[count:]):
        target[...] = source[...]


def shards(ring, rounds, queries, image_keys, image_values, cotangent, gate, tile_list, slot_range):
    keys, values = image_keys[0, 0], image_values[0, 0]
    tanh = jnp.tanh(gate)
    any_spec = pl.BlockSpec(memory_space=pl.ANY)
    smem_spec = pl.BlockSpec(memory_space=pltpu.SMEM)
    tail_rows = KEYS_ROWS - KEYS_MAIN
    tail_spec = pl.BlockSpec((tail_rows, KV * HD), lambda i: (KEYS_MAIN // tail_rows, 0))
    vmem_spec = pl.BlockSpec(memory_space=pltpu.VMEM)
    sems = lambda *shape: pltpu.SemaphoreType.DMA(shape)
    total_rounds = rounds[0] + rounds[1]
    attended, query_grad, key_out, value_out, gate_out = pl.pallas_call(
        functools.partial(kernel, ring, rounds),
        out_shape=(
            jax.ShapeDtypeStruct((BLK, KV * WIDTH), BF16),
            jax.ShapeDtypeStruct((BLK, KV * WIDTH), BF16),
            jax.ShapeDtypeStruct((KEYS_ROWS, KV * HD), BF16),
            jax.ShapeDtypeStruct((KEYS_ROWS, KV * HD), BF16),
            jax.ShapeDtypeStruct((1, 1), F32),
        ),
        grid=(1,),
        in_specs=[smem_spec, smem_spec, vmem_spec, tail_spec, tail_spec] + [any_spec] * 4,
        out_specs=(any_spec,) * 4 + (smem_spec,),
        scratch_shapes=[
            pltpu.VMEM((3, 1, BLK), F32),
            pltpu.VMEM((1, ROWS), F32),
            pltpu.VMEM((3, KV, BLK, WIDTH), BF16),
            pltpu.VMEM((3, KV, BLK, WIDTH), BF16),
            pltpu.VMEM((KV, KEYS_WIDE, HD), BF16),
            pltpu.VMEM((KV, KEYS_WIDE, HD), BF16),
            pltpu.VMEM((KV, HD, KEYS_WIDE), BF16),
            pltpu.VMEM((KV, HD, KEYS_WIDE), BF16),
            pltpu.VMEM((2, KV, BLK, WIDTH), BF16),
            pltpu.VMEM((2, KV, BLK, WIDTH), BF16),
            pltpu.VMEM((KV, BLK, WIDTH), F32),
            pltpu.VMEM((SLOTS, PARTS, HD, ROWS), F32),
            pltpu.VMEM((SLOTS, PARTS, KEYS_ROWS, ROWS), F32),
            pltpu.VMEM((KEYS_ROWS, HD), F32),
            pltpu.VMEM((KEYS_ROWS, HD), F32),
            pltpu.VMEM((SLOTS, 4, GROUP, BLK), F32),
            pltpu.VMEM((3, KV, 4, GROUP, BLK), F32),
            pltpu.VMEM((2, KV, 4, GROUP, BLK), F32),
            pltpu.VMEM((KV, 2, GROUP, BLK), F32),
            pltpu.VMEM((2, KV, 2, GROUP, BLK), F32),
            pltpu.VMEM((3, GROUP, BLK), F32),
            pltpu.VMEM((SLOTS, PARTS, HD, ROWS), BF16),
            pltpu.VMEM((GROUP, BLK), F32),
            pltpu.VMEM((total_rounds, GROUP, BLK), F32),
            pltpu.VMEM((total_rounds, GROUP, BLK), F32),
            sems(2, KV),
            sems(2, KV),
            sems(2, 2, KV),
            sems(2, 2, KV),
            sems(2, 2, KV),
            sems(2, 2, KV),
            sems(2, 2, KV, PARTS),
            sems(2, 2, KV, PARTS),
            sems(2, KV),
            sems(2, KV),
            sems(2, total_rounds),
        ],
        compiler_params=pltpu.CompilerParams(
            collective_id=0, has_side_effects=True, vmem_limit_bytes=VMEM_LIMIT
        ),
        cost_estimate=pl.CostEstimate(
            flops=2 * 6 * UNITS * 1024 * KEYS * HD,
            bytes_accessed=11_000_000,
            transcendentals=UNITS * 1024 * KEYS,
        ),
    )(
        tanh.reshape(1, 1),
        tile_list[0].T,
        slot_range[0].T,
        keys,
        values,
        queries[0],
        cotangent[0],
        keys,
        values,
    )

    steps = 4
    rows = BLK // steps
    key_rows = -(-KEYS // (16 * steps)) * 16
    token_spec = pl.BlockSpec((rows, KV * WIDTH), lambda i: (i, 0))
    key_spec = pl.BlockSpec((key_rows, KV * HD), lambda i: (i, 0))
    specs = (token_spec, token_spec, key_spec, key_spec)
    attended, query_grad, key_grad, value_grad = pl.pallas_call(
        hand_on,
        out_shape=(
            jax.ShapeDtypeStruct((BLK, KV * WIDTH), BF16),
            jax.ShapeDtypeStruct((BLK, KV * WIDTH), BF16),
            jax.ShapeDtypeStruct((KEYS, KV * HD), BF16),
            jax.ShapeDtypeStruct((KEYS, KV * HD), BF16),
        ),
        grid=(steps,),
        in_specs=specs,
        out_specs=specs,
        compiler_params=pltpu.CompilerParams(vmem_limit_bytes=VMEM_LIMIT),
    )(attended, query_grad, key_out, value_out)
    return (
        attended[None],
        query_grad[None],
        key_grad[None, None],
        value_grad[None, None],
        gate_out.reshape(()),
    )


def solution(mesh):
    ring = mesh.shape["seq"]
    rounds = (ring.bit_length() - 1, mesh.shape["dp"].bit_length() - 1)
    in_specs = (
        P("dp", "seq", None),
        P("dp", "seq", None, None),
        P("dp", "seq", None, None),
        P("dp", "seq", None),
        P(),
        P("dp", None, None),
        P("dp", None, None),
    )
    out_specs = (
        P("dp", "seq", None),
        P("dp", "seq", None),
        P("dp", "seq", None, None),
        P("dp", "seq", None, None),
        P(),
    )
    return jax.shard_map(
        functools.partial(shards, ring, rounds),
        mesh=mesh,
        in_specs=in_specs,
        out_specs=out_specs,
        check_vma=False,
    )
```

```python
import functools

import jax
import jax.numpy as jnp
from jax import lax
from jax.experimental import pallas as pl
from jax.experimental.pallas import tpu as pltpu
from jax.sharding import PartitionSpec as P

KV = 4
GROUP = 8
HD = 128
BLK = 128
KEYS = 1601
KEYS_MAIN = 1600
KEYS_ROWS = 1616
KEYS_WIDE = 1664
WIDTH = GROUP * HD
HEADS = 4
PARTS = GROUP // HEADS
ROWS = HEADS * BLK
CUTS = ((0, 768), (768, 848))
UNITS = 3 * KV
LAG = 4
SLOTS = LAG + 1
FWD_SIDE = (2, 0, 1) * KV
BWD_SIDE = (2, 0, 1) * (KV - 1) + (0, 1, 2)
LOW = -1e30
VMEM_LIMIT = 64 * 1024 * 1024 - 65536
SCALE = HD**-0.5
LOG2E = 1.4426950408889634
FACTOR = SCALE * LOG2E
F32 = jnp.float32
BF16 = jnp.bfloat16
MESH = pl.DeviceIdType.MESH


def mm(a, b):
    return jnp.dot(a, b, preferred_element_type=F32)


def pieces(wide):
    return [wide[:, g * BLK : (g + 1) * BLK] for g in range(HEADS)]


def stack_rows(chunk):
    return jnp.concatenate(pieces(chunk), axis=0)


def turn(chunk):
    return jnp.concatenate([piece.T for piece in pieces(chunk)], axis=1)


def slot_tables():
    free, held, fwd, bwd = list(range(SLOTS)), {}, [], []
    for step in range(UNITS + LAG):
        if step < UNITS:
            held[step // 3, FWD_SIDE[step]] = free.pop(0)
            fwd.append(held[step // 3, FWD_SIDE[step]])
        if step >= LAG:
            old = step - LAG
            bwd.append(held.pop((old // 3, BWD_SIDE[old])))
            free.append(bwd[-1])
    return fwd, bwd


FWD_SLOT, BWD_SLOT = slot_tables()


def pick(table, index):
    found = jnp.int32(table[0])
    for place, value in enumerate(table[1:], 1):
        found = jnp.where(index == place, value, found)
    return found


def kernel(
    ring,
    rounds,
    gate_ref,
    list_ref,
    range_ref,
    ktail_ref,
    vtail_ref,
    q_hbm,
    cot_hbm,
    k_hbm,
    v_hbm,
    att_hbm,
    dq_hbm,
    dk_hbm,
    dv_hbm,
    gsum_ref,
    mask_ref,
    rmax,
    qb,
    cb,
    kp,
    vp,
    kt,
    vt,
    ret_o,
    ret_q,
    own_o,
    onum,
    pbuf,
    dk_acc,
    dv_acc,
    stats,
    stats_out,
    stats_in,
    lse_out,
    lse_in,
    cvec,
    dot,
    gacc,
    gsend,
    grecv,
    s_kv,
    s_own,
    s_q,
    s_c,
    s_stat,
    s_lse,
    s_ro,
    s_rq,
    s_out,
    s_kvout,
    s_g,
):
    me = lax.axis_index("seq")
    dpi = lax.axis_index("dp")
    right = lax.rem(me + 1, ring)
    left = lax.rem(me + ring - 1, ring)
    tanh = gate_ref[0, 0]

    def cols(h):
        return pl.ds(pl.multiple_of(h * WIDTH, WIDTH), WIDTH)

    def to_side(d):
        return right if d == 0 else left

    def send_q(d, h):
        return pltpu.make_async_remote_copy(
            src_ref=q_hbm.at[:, cols(h)],
            dst_ref=qb.at[d, h],
            send_sem=s_q.at[0, d, h],
            recv_sem=s_q.at[1, d, h],
            device_id={"seq": to_side(d)},
            device_id_type=MESH,
        )

    def send_c(d, h):
        return pltpu.make_async_remote_copy(
            src_ref=cot_hbm.at[:, cols(h)],
            dst_ref=cb.at[d, h],
            send_sem=s_c.at[0, d, h],
            recv_sem=s_c.at[1, d, h],
            device_id={"seq": to_side(d)},
            device_id_type=MESH,
        )

    def send_stat(p, h):
        return pltpu.make_async_remote_copy(
            src_ref=stats_out.at[p, h],
            dst_ref=stats_in.at[1 - p, h],
            send_sem=s_stat.at[0, p, h],
            recv_sem=s_stat.at[1, 1 - p, h],
            device_id={"seq": to_side(1 - p)},
            device_id_type=MESH,
        )

    def send_lse(d, h):
        return pltpu.make_async_remote_copy(
            src_ref=lse_out.at[h],
            dst_ref=lse_in.at[d, h],
            send_sem=s_lse.at[0, d, h],
            recv_sem=s_lse.at[1, d, h],
            device_id={"seq": to_side(d)},
            device_id_type=MESH,
        )

    def chunk_lanes(c):
        return pl.ds(pl.multiple_of(c * ROWS, ROWS), ROWS)

    def send_ro(p, h, c):
        return pltpu.make_async_remote_copy(
            src_ref=cb.at[p, h, :, chunk_lanes(c)],
            dst_ref=ret_o.at[1 - p, h, :, chunk_lanes(c)],
            send_sem=s_ro.at[0, p, h, c],
            recv_sem=s_ro.at[1, 1 - p, h, c],
            device_id={"seq": to_side(1 - p)},
            device_id_type=MESH,
        )

    def send_rq(p, h, c):
        return pltpu.make_async_remote_copy(
            src_ref=qb.at[p, h, :, chunk_lanes(c)],
            dst_ref=ret_q.at[1 - p, h, :, chunk_lanes(c)],
            send_sem=s_rq.at[0, p, h, c],
            recv_sem=s_rq.at[1, 1 - p, h, c],
            device_id={"seq": to_side(1 - p)},
            device_id_type=MESH,
        )

    def gate_partner(r):
        name, place, bit = ("seq", me, r) if r < rounds[0] else ("dp", dpi, r - rounds[0])
        stride = 1 << bit
        return {name: place + stride * (1 - 2 * ((place // stride) % 2))}

    def send_gate(r):
        return pltpu.make_async_remote_copy(
            src_ref=gsend.at[r],
            dst_ref=grecv.at[r],
            send_sem=s_g.at[0, r],
            recv_sem=s_g.at[1, r],
            device_id=gate_partner(r),
            device_id_type=MESH,
        )

    own_q = lambda h: pltpu.make_async_copy(q_hbm.at[:, cols(h)], qb.at[2, h], s_own.at[0, h])
    own_c = lambda h: pltpu.make_async_copy(cot_hbm.at[:, cols(h)], cb.at[2, h], s_own.at[1, h])

    def load_kv(which, h):
        src, dst = ((k_hbm, kp), (v_hbm, vp))[which]
        lanes = pl.ds(pl.multiple_of(h * HD, HD), HD)
        return pltpu.make_async_copy(
            src.at[pl.ds(0, KEYS_MAIN), lanes],
            dst.at[h, pl.ds(0, KEYS_MAIN)],
            s_kv.at[which, h],
        )

    def store_kv(which, h):
        src, dst = ((kp, dk_hbm), (vp, dv_hbm))[which]
        return pltpu.make_async_copy(
            src.at[h, pl.ds(0, KEYS_ROWS)],
            dst.at[:, pl.ds(pl.multiple_of(h * HD, HD), HD)],
            s_kvout.at[which, h],
        )

    def store_att(h):
        return pltpu.make_async_copy(cb.at[2, h], att_hbm.at[:, cols(h)], s_out.at[0, h])

    def store_dq(h):
        return pltpu.make_async_copy(qb.at[2, h], dq_hbm.at[:, cols(h)], s_out.at[1, h])

    for h in range(KV):
        for which in range(2):
            load_kv(which, h).start()
    for h in range(KV):
        own_q(h).start()
        own_c(h).start()

    total_rounds = rounds[0] + rounds[1]
    barrier = pltpu.get_barrier_semaphore()
    for side in (left, right):
        pl.semaphore_signal(barrier, inc=1, device_id={"seq": side}, device_id_type=MESH)
    for r in range(total_rounds):
        pl.semaphore_signal(barrier, inc=1, device_id=gate_partner(r), device_id_type=MESH)
    pl.semaphore_wait(barrier, 2 + total_rounds)

    for send in (send_q, send_c):
        for d in range(2):
            send(d, 0).start()

    gacc[...] = jnp.zeros_like(gacc)
    for p, (block, slot) in enumerate(((left, 1), (right, 1), (me, 0))):
        tokens = pl.ds(pl.multiple_of(block * BLK, BLK), BLK)
        first, last = range_ref[0:1, tokens], range_ref[1:2, tokens]
        listed = jnp.where(list_ref[slot, block] == me, 1.0, 0.0).astype(F32)
        mask_ref[p] = jnp.where((first <= slot) & (slot < last), 1.0, 0.0).astype(F32) * listed

    def prepare(h, _):
        for which in range(2):
            load_kv(which, h).wait()
        lanes = pl.ds(pl.multiple_of(h * HD, HD), HD)
        for tail, dst, flipped in ((ktail_ref, kp, kt), (vtail_ref, vp, vt)):
            rows = lax.broadcasted_iota(jnp.int32, (KEYS_ROWS - KEYS_MAIN, HD), 0)
            dst[h, KEYS_MAIN:KEYS_ROWS, :] = jnp.where(
                rows < KEYS - KEYS_MAIN, tail[:, lanes].astype(F32), 0.0
            ).astype(BF16)
            dst[h, KEYS_ROWS:, :] = jnp.zeros((KEYS_WIDE - KEYS_ROWS, HD), BF16)
            for j in range(KEYS_WIDE // HD):
                piece = dst[h, j * HD : (j + 1) * HD, :]
                flipped[h, :, j * HD : (j + 1) * HD] = piece.T
        return 0

    lax.fori_loop(0, KV, prepare, 0)

    def combine(h):
        send_stat(0, h).wait_recv()
        send_stat(1, h).wait_recv()
        mine = stats_out[2, h]
        low = stats_in[0, h]
        high = stats_in[1, h]
        top = jnp.maximum(jnp.maximum(mine[0], low[0]), high[0])
        shares = [one[1] * jnp.exp2(one[0] - top) for one in (mine, low, high)]
        whole = shares[0] + shares[1] + shares[2]
        some = whole > 0.0
        safe = jnp.where(some, whole, 1.0)
        delta = (shares[0] * mine[2] + shares[1] * low[2] + shares[2] * high[2]) / safe
        gamma = (shares[0] * mine[3] + shares[1] * low[3] + shares[2] * high[3]) / safe
        lse_out[h, 0] = jnp.where(some, top + jnp.log(safe) * LOG2E, 0.0)
        lse_out[h, 1] = jnp.where(some, delta, 0.0)
        gacc[...] += jnp.where(some, gamma, 0.0)
        for d in range(2):
            send_lse(d, h).start()

    def finalize(h):
        for p in range(2):
            for c in range(PARTS):
                send_ro(p, h, c).wait_recv()
                send_rq(p, h, c).wait_recv()
        cb[2, h] = (own_o[h] + ret_o[0, h].astype(F32) + ret_o[1, h].astype(F32)).astype(BF16)
        qb[2, h] = (
            qb[2, h].astype(F32) + ret_q[0, h].astype(F32) + ret_q[1, h].astype(F32)
        ).astype(BF16)
        store_att(h).start()
        store_dq(h).start()

    def side_of(u):
        return lax.rem(u + 2, 3)

    def back_side(u):
        return lax.rem(jnp.where(u < UNITS - 3, u + 2, u), 3)

    def chunk(u, c, scoring, weighing, backing):
        if scoring:
            ahead = jnp.int32(0) if not weighing else jnp.minimum(u * PARTS + c + 1, UNITS * PARTS - 1)
            ua, ca = ahead // PARTS, lax.rem(ahead, PARTS)
            ha, pa = ua // 3, side_of(ua)
            slota = pick(FWD_SLOT, ua)
            query_ahead = turn(qb[pa, ha, :, chunk_lanes(ca)])
            next_max = None
        if weighing:
            h, p, slot = u // 3, side_of(u), pick(FWD_SLOT, u)
            row_max = rmax[...]
            total = jnp.zeros((1, ROWS), F32)
            out = jnp.zeros((HD, ROWS), F32)
        if backing:
            ub = u - LAG
            hb, pb, slotb = ub // 3, back_side(ub), pick(BWD_SLOT, ub)
            lanes = chunk_lanes(c)
            query = stack_rows(qb[pb, hb, :, lanes])
            grad = (tanh * stack_rows(cb[pb, hb, :, lanes]).astype(F32)).astype(BF16)
            grad_t = dot[slotb, c]
            lse, delta, weight = (
                jnp.concatenate(
                    [cvec[i, pl.ds(HEADS * c + g, 1), :] for g in range(HEADS)], axis=1
                )
                for i in range(3)
            )
            turned = jnp.zeros((HD, ROWS), F32)
        for start, size in CUTS:
            keys = slice(start, start + size)
            if backing:
                probs = jnp.exp2(pbuf[slotb, c, keys, :] - lse)
                prob_grad = mm(vp[hb, keys, :], grad_t)
                score_grad = (probs * (prob_grad - delta)).astype(BF16)
                dv_acc[keys, :] += mm(probs.astype(BF16), grad)
                dk_acc[keys, :] += mm(score_grad, query)
                turned = turned + mm(kt[hb, :, keys], score_grad)
            if weighing:
                fresh = jnp.exp2(pbuf[slot, c, keys, :] - row_max)
                total = total + jnp.sum(fresh, axis=0, keepdims=True)
                out = out + mm(vt[h, :, keys], fresh.astype(BF16))
            if scoring:
                scores = mm(kp[ha, keys, :], query_ahead) * FACTOR
                if start + size > KEYS:
                    position = lax.broadcasted_iota(jnp.int32, scores.shape, 0)
                    scores = jnp.where(position < KEYS - start, scores, LOW)
                pbuf[slota, ca, keys, :] = scores
                part = jnp.max(scores, axis=0, keepdims=True)
                next_max = part if next_max is None else jnp.maximum(next_max, part)
        if weighing:
            onum[slot, c] = out
            cot = turn(cb[p, h, :, chunk_lanes(c)].astype(F32))
            fresh_grad = (tanh * cot).astype(BF16)
            dot[slot, c] = fresh_grad
            deltas = jnp.sum(fresh_grad.astype(F32) * out, axis=0, keepdims=True) / total
            gammas = jnp.sum(cot * out, axis=0, keepdims=True) / total
            for kind, row in enumerate((row_max, total, deltas, gammas)):
                for g, piece in enumerate(pieces(row)):
                    stats[slot, kind, pl.ds(HEADS * c + g, 1), :] = piece
        if scoring:
            rmax[...] = next_max
        if backing:
            turned = turned * SCALE
            part = onum[slotb, c] * (weight * tanh)
            part = turn(part)
            qb[pb, hb, :, lanes] = turn(turned).astype(BF16)

            for d in range(2):

                @pl.when(pb == d)
                def _():
                    cb[d, hb, :, lanes] = part.astype(BF16)
                    send_ro(d, hb, c).start()
                    send_rq(d, hb, c).start()

            @pl.when(pb == 2)
            def _():
                own_o[hb, :, lanes] = part

    def wait_query(u):
        h, p = u // 3, side_of(u)
        for d in range(2):

            @pl.when(p == d)
            def _():
                send_q(d, h).wait_recv()

        @pl.when(p == 2)
        def _():
            own_q(h).wait()

    def wait_cotangent(u):
        h, p = u // 3, side_of(u)
        for d in range(2):

            @pl.when(p == d)
            def _():
                send_c(d, h).wait_recv()

        @pl.when(p == 2)
        def _():
            own_c(h).wait()

        for later, place, sends in (
            (1, 1, (send_q, send_c)),
            (2, 4, (send_q, send_c)),
            (3, 5, (send_q,)),
            (3, 6, (send_c,)),
        ):

            @pl.when(u == place)
            def _():
                for send in sends:
                    for d in range(2):
                        send(d, later).start()

    def forward_end(u):
        h, p, slot = u // 3, side_of(u), pick(FWD_SLOT, u)
        on = mask_ref[p] > 0.0
        for kind, fill in enumerate((LOW, 0.0, 0.0, 0.0)):
            stats_out[p, h, kind] = jnp.where(on, stats[slot, kind], fill)
        for d in range(2):

            @pl.when(p == d)
            def _():
                send_stat(d, h).start()

    def backward_start(u):
        h, p, slot = u // 3, back_side(u), pick(BWD_SLOT, u)

        def meet(lse, delta):
            on = mask_ref[p] > 0.0
            cvec[0] = jnp.where(on, lse, -LOW)
            cvec[1] = delta
            cvec[2] = jnp.where(on, jnp.exp2(stats[slot, 0] - lse), 0.0)

        for d in range(2):

            @pl.when(p == d)
            def _():
                send_lse(d, h).wait_recv()
                meet(lse_in[d, h, 0], lse_in[d, h, 1])

        @pl.when(p == 2)
        def _():
            meet(lse_out[h, 0], lse_out[h, 1])

        @pl.when(lax.rem(u, 3) == 0)
        def _():
            dk_acc[...] = jnp.zeros_like(dk_acc)
            dv_acc[...] = jnp.zeros_like(dv_acc)

    def backward_end(u):
        h = u // 3

        @pl.when(lax.rem(u, 3) == 2)
        def _():
            kp[h, :KEYS_ROWS, :] = (dk_acc[...] * SCALE).astype(BF16)
            vp[h, :KEYS_ROWS, :] = dv_acc[...].astype(BF16)
            for which in range(2):
                store_kv(which, h).start()

    def chunk_events(u, c):
        @pl.when((u >= 3) & (u <= UNITS) & (u % 3 == 0) & (c == PARTS // 2))
        def _():
            combine(u // 3 - 1)

    def step_events(u):
        @pl.when((u >= 9) & (u % 3 == 0))
        def _():
            finalize(u // 3 - 3)

    def step(u, backing):
        step_events(u)
        wait_cotangent(u)
        if backing:
            backward_start(u - LAG)

        def one(c, x):
            chunk_events(u, c)

            @pl.when((c == PARTS - 1) & (u < UNITS - 1))
            def _():
                wait_query(u + 1)

            chunk(u, c, True, True, backing)
            return x

        lax.fori_loop(0, PARTS, one, 0)
        forward_end(u)
        if backing:
            backward_end(u - LAG)
        return 0

    def gate_round(r):
        if r > 0:
            send_gate(r - 1).wait_recv()
            gacc[...] += grecv[r - 1]
        if r < total_rounds:
            gsend[r] = gacc[...]
            send_gate(r).start()

    def tail_step(u, _):
        step_events(u)
        backward_start(u - LAG)

        def one(c, x):
            chunk_events(u, c)
            chunk(u, c, False, False, True)
            place = (u - UNITS) * PARTS + c
            for r in range(total_rounds):

                @pl.when(place == 1 + r)
                def _():
                    gate_round(r)

            return x

        lax.fori_loop(0, PARTS, one, 0)
        backward_end(u - LAG)
        return 0

    wait_query(jnp.int32(0))
    chunk(0, 0, True, False, False)
    lax.fori_loop(0, LAG, lambda u, x: step(u, False), 0)
    lax.fori_loop(LAG, UNITS, lambda u, x: step(u, True), 0)
    lax.fori_loop(UNITS, UNITS + LAG, tail_step, 0)
    gate_round(total_rounds)
    finalize(KV - 1)
    gsum_ref[0, 0] = (1.0 - tanh * tanh) * jnp.sum(gacc[...])

    for r in range(total_rounds):
        send_gate(r).wait_send()
    for h in range(KV):
        for d in range(2):
            send_q(d, h).wait_send()
            send_c(d, h).wait_send()
            send_stat(d, h).wait_send()
            send_lse(d, h).wait_send()
            for c in range(PARTS):
                send_ro(d, h, c).wait_send()
                send_rq(d, h, c).wait_send()
            store_kv(d, h).wait()
        store_att(h).wait()
        store_dq(h).wait()


def hand_on(*refs):
    count = len(refs) // 2
    for source, target in zip(refs[:count], refs[count:]):
        target[...] = source[...]


def shards(ring, rounds, queries, image_keys, image_values, cotangent, gate, tile_list, slot_range):
    keys, values = image_keys[0, 0], image_values[0, 0]
    tanh = jnp.tanh(gate)
    any_spec = pl.BlockSpec(memory_space=pl.ANY)
    smem_spec = pl.BlockSpec(memory_space=pltpu.SMEM)
    tail_rows = KEYS_ROWS - KEYS_MAIN
    tail_spec = pl.BlockSpec((tail_rows, KV * HD), lambda i: (KEYS_MAIN // tail_rows, 0))
    vmem_spec = pl.BlockSpec(memory_space=pltpu.VMEM)
    sems = lambda *shape: pltpu.SemaphoreType.DMA(shape)
    total_rounds = rounds[0] + rounds[1]
    attended, query_grad, key_out, value_out, gate_out = pl.pallas_call(
        functools.partial(kernel, ring, rounds),
        out_shape=(
            jax.ShapeDtypeStruct((BLK, KV * WIDTH), BF16),
            jax.ShapeDtypeStruct((BLK, KV * WIDTH), BF16),
            jax.ShapeDtypeStruct((KEYS_ROWS, KV * HD), BF16),
            jax.ShapeDtypeStruct((KEYS_ROWS, KV * HD), BF16),
            jax.ShapeDtypeStruct((1, 1), F32),
        ),
        grid=(1,),
        in_specs=[smem_spec, smem_spec, vmem_spec, tail_spec, tail_spec] + [any_spec] * 4,
        out_specs=(any_spec,) * 4 + (smem_spec,),
        scratch_shapes=[
            pltpu.VMEM((3, 1, BLK), F32),
            pltpu.VMEM((1, ROWS), F32),
            pltpu.VMEM((3, KV, BLK, WIDTH), BF16),
            pltpu.VMEM((3, KV, BLK, WIDTH), BF16),
            pltpu.VMEM((KV, KEYS_WIDE, HD), BF16),
            pltpu.VMEM((KV, KEYS_WIDE, HD), BF16),
            pltpu.VMEM((KV, HD, KEYS_WIDE), BF16),
            pltpu.VMEM((KV, HD, KEYS_WIDE), BF16),
            pltpu.VMEM((2, KV, BLK, WIDTH), BF16),
            pltpu.VMEM((2, KV, BLK, WIDTH), BF16),
            pltpu.VMEM((KV, BLK, WIDTH), F32),
            pltpu.VMEM((SLOTS, PARTS, HD, ROWS), F32),
            pltpu.VMEM((SLOTS, PARTS, KEYS_ROWS, ROWS), F32),
            pltpu.VMEM((KEYS_ROWS, HD), F32),
            pltpu.VMEM((KEYS_ROWS, HD), F32),
            pltpu.VMEM((SLOTS, 4, GROUP, BLK), F32),
            pltpu.VMEM((3, KV, 4, GROUP, BLK), F32),
            pltpu.VMEM((2, KV, 4, GROUP, BLK), F32),
            pltpu.VMEM((KV, 2, GROUP, BLK), F32),
            pltpu.VMEM((2, KV, 2, GROUP, BLK), F32),
            pltpu.VMEM((3, GROUP, BLK), F32),
            pltpu.VMEM((SLOTS, PARTS, HD, ROWS), BF16),
            pltpu.VMEM((GROUP, BLK), F32),
            pltpu.VMEM((total_rounds, GROUP, BLK), F32),
            pltpu.VMEM((total_rounds, GROUP, BLK), F32),
            sems(2, KV),
            sems(2, KV),
            sems(2, 2, KV),
            sems(2, 2, KV),
            sems(2, 2, KV),
            sems(2, 2, KV),
            sems(2, 2, KV, PARTS),
            sems(2, 2, KV, PARTS),
            sems(2, KV),
            sems(2, KV),
            sems(2, total_rounds),
        ],
        compiler_params=pltpu.CompilerParams(
            collective_id=0, has_side_effects=True, vmem_limit_bytes=VMEM_LIMIT
        ),
        cost_estimate=pl.CostEstimate(
            flops=2 * 6 * UNITS * 1024 * KEYS * HD,
            bytes_accessed=11_000_000,
            transcendentals=UNITS * 1024 * KEYS,
        ),
    )(
        tanh.reshape(1, 1),
        tile_list[0].T,
        slot_range[0].T,
        keys,
        values,
        queries[0],
        cotangent[0],
        keys,
        values,
    )

    steps = 4
    rows = BLK // steps
    key_rows = -(-KEYS // (16 * steps)) * 16
    token_spec = pl.BlockSpec((rows, KV * WIDTH), lambda i: (i, 0))
    key_spec = pl.BlockSpec((key_rows, KV * HD), lambda i: (i, 0))
    specs = (token_spec, token_spec, key_spec, key_spec)
    attended, query_grad, key_grad, value_grad = pl.pallas_call(
        hand_on,
        out_shape=(
            jax.ShapeDtypeStruct((BLK, KV * WIDTH), BF16),
            jax.ShapeDtypeStruct((BLK, KV * WIDTH), BF16),
            jax.ShapeDtypeStruct((KEYS, KV * HD), BF16),
            jax.ShapeDtypeStruct((KEYS, KV * HD), BF16),
        ),
        grid=(steps,),
        in_specs=specs,
        out_specs=specs,
        compiler_params=pltpu.CompilerParams(vmem_limit_bytes=VMEM_LIMIT),
    )(attended, query_grad, key_out, value_out)
    return (
        attended[None],
        query_grad[None],
        key_grad[None, None],
        value_grad[None, None],
        gate_out.reshape(()),
    )


def solution(mesh):
    ring = mesh.shape["seq"]
    rounds = (ring.bit_length() - 1, mesh.shape["dp"].bit_length() - 1)
    in_specs = (
        P("dp", "seq", None),
        P("dp", "seq", None, None),
        P("dp", "seq", None, None),
        P("dp", "seq", None),
        P(),
        P("dp", None, None),
        P("dp", None, None),
    )
    out_specs = (
        P("dp", "seq", None),
        P("dp", "seq", None),
        P("dp", "seq", None, None),
        P("dp", "seq", None, None),
        P(),
    )
    return jax.shard_map(
        functools.partial(shards, ring, rounds),
        mesh=mesh,
        in_specs=in_specs,
        out_specs=out_specs,
        check_vma=False,
    )
```
